256 devices in a mesh: seq: 8 (over y, core), exp: 32 (over z, x).
Axes of the slice: x: 4, y: 4, z: 8, core: 2. Of those that a mesh axis runs over, the one named last changes fastest.
Arguments:
- tokens: bfloat16 [32, 4096, 1280], P('exp', 'seq'), may hold values from -64 to 64
- router: bfloat16 [1280, 64], replicated, may hold values from -2 to 2
- w_in: bfloat16 [32, 1280, 5120], P('exp', None, 'seq'), may hold values from -0.15625 to 0.15625
- w_out: bfloat16 [32, 5120, 1280], P('exp', 'seq'), may hold values from -0.078125 to 0.078125
- grad_out: bfloat16 [32, 4096, 1280], P('exp', 'seq'), may hold values from -6 to 6
Outputs:
- mixed: bfloat16 [32, 4096, 1280], P('exp', 'seq')
- d_tokens: bfloat16 [32, 4096, 1280], P('exp', 'seq')
- d_router: float32 [1280, 64], P(('seq', 'exp'))
- d_w_in: bfloat16 [32, 1280, 5120], P('exp', None, 'seq')
- d_w_out: bfloat16 [32, 5120, 1280], P('exp', 'seq')
The draws below stay inside these ranges and needn't reach their ends.
All inputs are finite; a program needn't handle non-finite values.
Results may differ from the reference program's by a relative error of at most 0.034.
Values may be sent and summed in bfloat16 or wider, within the bound.
A program may use at most 64 MiB of HBM per device.

```python
import math
import jax
import jax.numpy as jnp
from jax import lax

MODEL_WIDTH = 1280
FF = 5120
SLOTS_PER_EXPERT = 2
EXPERT_COUNT = 32
TOTAL_SLOTS = 64
CLIP_COUNT = 32
LEN = 4096


def shared_normal(key):
    return jnp.clip(jax.random.normal(key, (MODEL_WIDTH, TOTAL_SLOTS), jnp.float32), -4.0, 4.0)


def draw_router(key, part):
    base = shared_normal(key)
    return (2.5 * base / math.sqrt(MODEL_WIDTH)).astype(jnp.bfloat16)


def draw_tokens(key, part):
    key = jax.random.fold_in(key, 7)
    split_random_keys = jax.random.split(key, 1)
    noise = jnp.clip(jax.random.normal(split_random_keys[0], (CLIP_COUNT, LEN, MODEL_WIDTH), jnp.float32), -6.0, 6.0)
    return noise.astype(jnp.bfloat16)


def levels(key, extent, cuts, low, high):
    loudness = 1.0
    for axis_at, parts in cuts:
        steps = jax.random.uniform(jax.random.fold_in(jax.random.fold_in(key, 6), axis_at), (parts,), jnp.float32, low / len(cuts), high / len(cuts))
        loudness = loudness * jnp.repeat(jnp.exp(steps), extent[axis_at] // parts).reshape((-1,) + (1,) * (len(extent) - 1 - axis_at))
    return loudness


def bell_draw(rng, dims, scale, most, cuts=(), kind=jnp.bfloat16):
    array = jax.random.normal(rng, dims, jnp.float32) * scale
    if len(cuts) > 0:
        array = levels(rng, dims, cuts, -0.22, 0.18) * array
    return jnp.clip(array, min=-most, max=most).astype(kind)


def setup_inputs(seed: int = 0) -> dict:
    splits = jax.random.split(jax.random.key(seed), 6)
    tokens = draw_tokens(jax.random.fold_in(splits[5], 71), 0)
    router = draw_router(jax.random.fold_in(splits[5], 71), 0)
    w_in = bell_draw(splits[2], (EXPERT_COUNT, MODEL_WIDTH, FF), MODEL_WIDTH ** -0.5, 0.15625, ((0, 32), (2, 8)))
    w_out = bell_draw(splits[3], (EXPERT_COUNT, FF, MODEL_WIDTH), FF ** -0.5, 0.078125, ((0, 32), (1, 8)))
    grad_out = bell_draw(splits[4], (CLIP_COUNT, LEN, MODEL_WIDTH), 1.0, 6.0, ((0, 32), (1, 8)))
    return {"tokens": tokens, "router": router, "w_in": w_in, "w_out": w_out, "grad_out": grad_out}


def gelu_grad(values):
    return 0.5 * (1.0 + lax.erf(values * (1.0 / math.sqrt(2.0)))) + values * jnp.exp(-0.5 * values * values) / math.sqrt(2.0 * math.pi)

def reference(tokens, router, w_in, w_out, grad_out):
    feats = tokens.astype(jnp.float32)
    phi = router.astype(jnp.float32)
    logits = jnp.einsum('ctd,dj->cjt', feats, phi)
    col_top = lax.optimization_barrier(jnp.max(logits, axis=2, keepdims=True))
    col_exp = jnp.exp(logits - col_top)
    dispatch = col_exp / lax.optimization_barrier(jnp.sum(col_exp, axis=2, keepdims=True))
    dispatch_b = dispatch.astype(jnp.bfloat16)
    slots_in = jnp.einsum('cjt,ctd->cjd', dispatch_b.astype(jnp.float32), feats).astype(jnp.bfloat16)
    rows = slots_in.reshape(CLIP_COUNT, EXPERT_COUNT, SLOTS_PER_EXPERT, MODEL_WIDTH).transpose(1, 0, 2, 3).reshape(EXPERT_COUNT, CLIP_COUNT * SLOTS_PER_EXPERT, MODEL_WIDTH)
    hidden = jnp.einsum('erd,edf->erf', rows.astype(jnp.float32), w_in.astype(jnp.float32))
    activated = jax.nn.gelu(hidden, approximate=False).astype(jnp.bfloat16)
    rows_per_expert = jnp.einsum('erf,efd->erd', activated.astype(jnp.float32), w_out.astype(jnp.float32)).astype(jnp.bfloat16)
    slot_output = rows_per_expert.reshape(EXPERT_COUNT, CLIP_COUNT, SLOTS_PER_EXPERT, MODEL_WIDTH).transpose(1, 0, 2, 3).reshape(CLIP_COUNT, TOTAL_SLOTS, MODEL_WIDTH)
    row_top = lax.optimization_barrier(jnp.max(logits, axis=1, keepdims=True))
    row_exp = jnp.exp(logits - row_top)
    combine = row_exp / lax.optimization_barrier(jnp.sum(row_exp, axis=1, keepdims=True))
    combine_b = combine.astype(jnp.bfloat16)
    slots_f = slot_output.astype(jnp.float32)
    mixed = jnp.einsum('cjt,cjd->ctd', combine_b.astype(jnp.float32), slots_f).astype(jnp.bfloat16)
    cotangent = grad_out.astype(jnp.float32)
    d_slots_out = jnp.einsum('cjt,ctd->cjd', combine_b.astype(jnp.float32), cotangent).astype(jnp.bfloat16)
    d_combine = jnp.einsum('cjd,ctd->cjt', slots_f, cotangent)
    d_logit_c = combine * (d_combine - lax.optimization_barrier(jnp.sum(combine * d_combine, axis=1, keepdims=True)))
    d_rows = d_slots_out.reshape(CLIP_COUNT, EXPERT_COUNT, SLOTS_PER_EXPERT, MODEL_WIDTH).transpose(1, 0, 2, 3).reshape(EXPERT_COUNT, CLIP_COUNT * SLOTS_PER_EXPERT, MODEL_WIDTH)
    d_rows_f = d_rows.astype(jnp.float32)
    d_activated = jnp.einsum('erd,efd->erf', d_rows_f, w_out.astype(jnp.float32))
    d_hidden = (d_activated * gelu_grad(hidden)).astype(jnp.bfloat16)
    d_w_out = jnp.einsum('erf,erd->efd', activated.astype(jnp.float32), d_rows_f).astype(jnp.bfloat16)
    d_w_in = jnp.einsum('erd,erf->edf', rows.astype(jnp.float32), d_hidden.astype(jnp.float32)).astype(jnp.bfloat16)
    input_rows_gradient = jnp.einsum('erf,edf->erd', d_hidden.astype(jnp.float32), w_in.astype(jnp.float32)).astype(jnp.bfloat16)
    slot_input_gradient = input_rows_gradient.reshape(EXPERT_COUNT, CLIP_COUNT, SLOTS_PER_EXPERT, MODEL_WIDTH).transpose(1, 0, 2, 3).reshape(CLIP_COUNT, TOTAL_SLOTS, MODEL_WIDTH)
    d_slots_f = slot_input_gradient.astype(jnp.float32)
    d_dispatch = jnp.einsum('cjd,ctd->cjt', d_slots_f, feats)
    d_logit_d = dispatch * (d_dispatch - lax.optimization_barrier(jnp.sum(dispatch * d_dispatch, axis=2, keepdims=True)))
    d_logit_b = (d_logit_c + d_logit_d).astype(jnp.bfloat16)
    d_logit_f = d_logit_b.astype(jnp.float32)
    d_tokens = (jnp.einsum('cjt,cjd->ctd', dispatch_b.astype(jnp.float32), d_slots_f) + jnp.einsum('cjt,dj->ctd', d_logit_f, phi)).astype(jnp.bfloat16)
    d_router = jnp.einsum('ctd,cjt->dj', feats, d_logit_f)
    return (mixed, d_tokens, d_router, d_w_in, d_w_out)
```

```python
import math

import jax
import jax.numpy as jnp
from jax import lax
from jax.experimental import pallas as pl
from jax.experimental.pallas import tpu as pltpu
from jax.sharding import PartitionSpec as P

F32 = jnp.float32
BF16 = jnp.bfloat16
MESH = pl.DeviceIdType.MESH
SEQ = 8
EXP = 32
XS = 4
D = 1280
H = 640
T = 512
S = 64


def nn(a, b):
    return lax.dot_general(a, b, (((1,), (0,)), ((), ())), preferred_element_type=F32)


def nt(a, b):
    return lax.dot_general(a, b, (((1,), (1,)), ((), ())), preferred_element_type=F32)


def fold(a):
    lo = a[:, :H].reshape(SEQ, 8, H)
    hi = a[:, H:].reshape(SEQ, 8, H)
    return jnp.concatenate([lo, hi], axis=1).astype(BF16)


def unfold(a):
    a = a.astype(F32)
    lo = a[:, :8].reshape(S, H)
    hi = a[:, 8:].reshape(S, H)
    return jnp.concatenate([lo, hi], axis=1).astype(BF16)


def column_to_rows(top, low):
    square = jnp.concatenate(
        [jnp.broadcast_to(top, (S, 128)), jnp.broadcast_to(low, (S, 128))], axis=0
    )
    return square.T[:8]


def rows_to_column(rows):
    return jnp.concatenate([rows] * 16, axis=0).T


def kernel(
    tokens_hbm, router_hbm, w_in_hbm, w_out_hbm, grad_hbm,
    mixed_hbm, d_tokens_hbm, d_router_hbm, d_w_in_hbm, d_w_out_hbm,
    tok, rout, w_in, w_out, grad, mixed_v, d_tok_v, d_rout_v, d_w_in_v, d_w_out_v,
    rs_send, rs_recv, ex_send, ex_recv, ag, stat_send, stat_recv, col_send, col_recv,
    r1_send, r1_recv, r1_sum, r2_send, r2_recv,
    in_sem, out_sem, rs_ss, rs_rs, ex_ss, ex_rs, ag_ss, ag_rs, st_ss, st_rs, r_ss, r_rs,
):
    me_s = lax.axis_index("seq")
    me_n = lax.axis_index("exp")
    z = me_n // XS
    x = lax.rem(me_n, XS)
    partner = lax.rem(me_s - z + SEQ, SEQ)

    loads = [
        pltpu.make_async_copy(src, dst, in_sem.at[i])
        for i, (src, dst) in enumerate(
            ((router_hbm, rout), (tokens_hbm, tok), (grad_hbm, grad), (w_out_hbm, w_out), (w_in_hbm, w_in))
        )
    ]
    for load in loads:
        load.start()

    barrier = pltpu.get_barrier_semaphore()

    def greet_seq(k, carry):
        pl.semaphore_signal(
            barrier, inc=1, device_id=(lax.rem(me_s + k, SEQ), me_n), device_id_type=MESH
        )
        return carry

    def greet_exp(k, carry):
        pl.semaphore_signal(
            barrier, inc=1, device_id=(me_s, lax.rem(me_n + k, EXP)), device_id_type=MESH
        )
        return carry

    lax.fori_loop(1, SEQ, greet_seq, 0)
    lax.fori_loop(1, EXP, greet_exp, 0)

    def over_seq(make):
        def step(k, carry):
            make(lax.rem(me_s + k, SEQ)).start()
            return carry

        lax.fori_loop(1, SEQ, step, 0)

    def all_of(ref, sem):
        pltpu.make_async_copy(ref, ref, sem).wait()

    def rs_start(i):
        rs_recv[i, me_s] = rs_send[i, partner]
        over_seq(
            lambda p: pltpu.make_async_remote_copy(
                src_ref=rs_send.at[i, lax.rem(p - z + SEQ, SEQ)],
                dst_ref=rs_recv.at[i, me_s],
                send_sem=rs_ss.at[i], recv_sem=rs_rs.at[i],
                device_id=(p, me_n), device_id_type=MESH,
            )
        )

    def rs_finish_ex_start(i):
        all_of(rs_recv.at[i, pl.ds(0, SEQ - 1)], rs_rs.at[i])
        total = rs_recv[i, 0].astype(F32)
        for k in range(1, SEQ):
            total = total + rs_recv[i, k].astype(F32)
        rows = jnp.concatenate([total[:8], total[8:]], axis=1)
        for k in range(XS):
            ex_send[i, k] = rows[2 * k : 2 * k + 2]
        for k in range(XS):
            to = XS * partner + k

            @pl.when(to != me_n)
            def _():
                pltpu.make_async_remote_copy(
                    src_ref=ex_send.at[i, k], dst_ref=ex_recv.at[i, x],
                    send_sem=ex_ss.at[i], recv_sem=ex_rs.at[i],
                    device_id=(me_s, to), device_id_type=MESH,
                ).start()

            @pl.when(to == me_n)
            def _():
                ex_recv[i, x] = ex_send[i, k]

    def ex_finish_ag_start(i):
        @pl.when(partner != z)
        def _():
            all_of(ex_recv.at[i], ex_rs.at[i])

        @pl.when(partner == z)
        def _():
            all_of(ex_recv.at[i, pl.ds(0, XS - 1)], ex_rs.at[i])

        rows = jnp.concatenate([ex_recv[i, k] for k in range(XS)], axis=0)
        ag[i, partner] = jnp.concatenate([rows[:, :H], rows[:, H:]], axis=0).astype(BF16)
        over_seq(
            lambda p: pltpu.make_async_remote_copy(
                src_ref=ag.at[i, partner], dst_ref=ag.at[i, partner],
                send_sem=ag_ss.at[i], recv_sem=ag_rs.at[i],
                device_id=(p, me_n), device_id_type=MESH,
            )
        )

    def ag_finish(i):
        all_of(ag.at[i, pl.ds(0, SEQ - 1)], ag_rs.at[i])
        return unfold(ag[i])

    def stat_start(i, send, recv):
        recv[me_s] = send[...]
        over_seq(
            lambda p: pltpu.make_async_remote_copy(
                src_ref=send, dst_ref=recv.at[me_s],
                send_sem=st_ss.at[i], recv_sem=st_rs.at[i],
                device_id=(p, me_n), device_id_type=MESH,
            )
        )

    loads[0].wait()
    router_t = rout[...].astype(F32).T.astype(BF16)
    loads[1].wait()
    logits = nt(router_t, tok[...])
    own_top = jnp.max(logits, axis=1, keepdims=True)
    own_exp = jnp.exp(logits - own_top)
    own_total = jnp.sum(own_exp, axis=1, keepdims=True)
    stat_send[...] = column_to_rows(own_top, own_total)
    pl.semaphore_wait(barrier, SEQ - 1 + EXP - 1)
    stat_start(0, stat_send, stat_recv)
    row_exp = jnp.exp(logits - jnp.max(logits, axis=0, keepdims=True))
    combine = row_exp / jnp.sum(row_exp, axis=0, keepdims=True)

    loads[2].wait()
    rs_send[0] = fold(nn(combine.astype(BF16), grad[...]))
    rs_start(0)
    in_part = nn(own_exp.astype(BF16), tok[...])
    all_of(stat_recv.at[pl.ds(0, SEQ - 1)], st_rs.at[0])
    stats = [stat_recv[k] for k in range(SEQ)]
    top = stats[0]
    for k in range(1, SEQ):
        top = jnp.maximum(top, stats[k])
    lane = lax.broadcasted_iota(jnp.int32, (8, 128), 1)
    top = jnp.where(lane < S, top, 0.0)
    total = jnp.zeros((8, 128), F32)
    for k in range(SEQ):
        shift = jnp.where(lane < S, stats[k] - top, 0.0)
        total = total + pltpu.roll(stats[k], S, 1) * jnp.exp(shift)
    merged = rows_to_column(jnp.where(lane < S, top, pltpu.roll(total, S, 1)))
    scale = jnp.exp(own_top - merged[:S, :1]) / merged[S:, :1]
    rs_send[1] = fold(in_part * scale)
    rs_start(1)
    dispatch = own_exp * scale

    rs_finish_ex_start(0)
    rs_finish_ex_start(1)
    ex_finish_ag_start(0)
    ex_finish_ag_start(1)

    loads[3].wait()
    d_rows = ag_finish(0)
    d_act = nt(d_rows, w_out[...])
    loads[4].wait()
    rows = ag_finish(1)
    hidden = nn(rows, w_in[...])
    cdf = 0.5 * (1.0 + lax.erf(hidden * (1.0 / math.sqrt(2.0))))
    act = hidden * cdf
    pdf = jnp.exp(-0.5 * hidden * hidden) * (1.0 / math.sqrt(2.0 * math.pi))
    d_hidden = d_act * (cdf + hidden * pdf)
    d_hidden_b = d_hidden.astype(BF16)
    rs_send[2] = fold(nt(d_hidden_b, w_in[...]))
    rs_start(2)
    rs_send[3] = fold(nn(act.astype(BF16), w_out[...]))
    rs_start(3)

    rs_finish_ex_start(2)
    rs_finish_ex_start(3)
    act_t = act.T.astype(BF16)
    for k in range(5):
        part = slice(128 * k, 128 * k + 128)
        d_w_out_v[part] = nn(act_t[part], d_rows).astype(BF16)
    out0 = pltpu.make_async_copy(d_w_out_v, d_w_out_hbm, out_sem.at[0])
    out0.start()
    ex_finish_ag_start(2)
    ex_finish_ag_start(3)
    rows_t = rows.astype(F32).T.astype(BF16)
    for k in range(10):
        part = slice(128 * k, 128 * k + 128)
        d_w_in_v[part] = nn(rows_t[part], d_hidden_b).astype(BF16)
    out1 = pltpu.make_async_copy(d_w_in_v, d_w_in_hbm, out_sem.at[1])
    out1.start()

    d_slots = ag_finish(2)
    d_dispatch = nt(d_slots, tok[...])
    weighted = dispatch * d_dispatch
    column = jnp.sum(weighted, axis=1, keepdims=True)
    col_send[...] = column_to_rows(column, column)
    stat_start(1, col_send, col_recv)
    slots_out = ag_finish(3)
    d_combine = nt(slots_out, grad[...])
    d_logit_c = combine * (d_combine - jnp.sum(combine * d_combine, axis=0, keepdims=True))
    combine_t = combine.T.astype(BF16)
    for k in range(4):
        part = slice(128 * k, 128 * k + 128)
        mixed_v[part] = nn(combine_t[part], slots_out).astype(BF16)
    out2 = pltpu.make_async_copy(mixed_v, mixed_hbm, out_sem.at[2])
    out2.start()
    all_of(col_recv.at[pl.ds(0, SEQ - 1)], st_rs.at[1])
    total = col_recv[0]
    for k in range(1, SEQ):
        total = total + col_recv[k]
    column_sum = rows_to_column(total)[:S, :1]
    d_logit = d_logit_c + dispatch * (d_dispatch - column_sum)

    d_router_t = nn(d_logit.astype(BF16), tok[...])
    pair = jnp.concatenate([d_router_t, pltpu.roll(d_router_t, D - 80, 1)], axis=0).T
    for k in range(SEQ):
        r1_send[k] = pair[160 * k : 160 * k + 80]
    r1_recv[me_s] = r1_send[me_s]
    over_seq(
        lambda p: pltpu.make_async_remote_copy(
            src_ref=r1_send.at[p], dst_ref=r1_recv.at[me_s],
            send_sem=r_ss.at[0], recv_sem=r_rs.at[0],
            device_id=(p, me_n), device_id_type=MESH,
        )
    )
    weights = jnp.concatenate([dispatch, d_logit], axis=0).T.astype(BF16)
    values = jnp.concatenate([d_slots, router_t], axis=0)
    for k in range(4):
        part = slice(128 * k, 128 * k + 128)
        d_tok_v[part] = nn(weights[part], values).astype(BF16)
    out3 = pltpu.make_async_copy(d_tok_v, d_tokens_hbm, out_sem.at[3])
    out3.start()
    all_of(r1_recv.at[pl.ds(0, SEQ - 1)], r_rs.at[0])
    total = r1_recv[0]
    for k in range(1, SEQ):
        total = total + r1_recv[k]
    r1_sum[0:80] = total
    r1_sum[80:88] = jnp.zeros((8, 128), F32)
    for k in range(16):
        r2_send[k] = r1_sum[5 * k : 5 * k + 8]
    r2_recv[me_n] = r2_send[lax.rem(me_n, 16)]

    def final(k, carry):
        to = lax.rem(me_n + k, EXP)
        pltpu.make_async_remote_copy(
            src_ref=r2_send.at[lax.rem(to, 16)], dst_ref=r2_recv.at[me_n],
            send_sem=r_ss.at[1], recv_sem=r_rs.at[1],
            device_id=(me_s, to), device_id_type=MESH,
        ).start()
        return carry

    lax.fori_loop(1, EXP, final, 0)
    all_of(r2_recv.at[pl.ds(0, EXP - 1)], r_rs.at[1])
    total = r2_recv[0]
    for k in range(1, EXP):
        total = total + r2_recv[k]
    high = me_n >= 16
    total = jnp.where(high, pltpu.roll(total, S, 1), total)
    d_rout_v[...] = total[:5, :S]
    out4 = pltpu.make_async_copy(d_rout_v, d_router_hbm, out_sem.at[4])
    out4.start()

    for i in range(4):
        all_of(rs_send.at[i, pl.ds(0, SEQ - 1)], rs_ss.at[i])

        @pl.when(partner != z)
        def _():
            all_of(ex_send.at[i], ex_ss.at[i])

        @pl.when(partner == z)
        def _():
            all_of(ex_send.at[i, pl.ds(0, XS - 1)], ex_ss.at[i])

        all_of(ag.at[i, pl.ds(0, SEQ - 1)], ag_ss.at[i])
    all_of(stat_recv.at[pl.ds(0, SEQ - 1)], st_ss.at[0])
    all_of(col_recv.at[pl.ds(0, SEQ - 1)], st_ss.at[1])
    all_of(r1_send.at[pl.ds(0, SEQ - 1)], r_ss.at[0])
    all_of(r2_recv.at[pl.ds(0, EXP - 1)], r_ss.at[1])
    for out in (out0, out1, out2, out3, out4):
        out.wait()


def shards(tokens, router, w_in, w_out, grad_out):
    any_space = pl.BlockSpec(memory_space=pl.ANY)
    dma = pltpu.SemaphoreType.DMA
    mixed, d_tokens, d_router, d_w_in, d_w_out = pl.pallas_call(
        kernel,
        out_shape=(
            jax.ShapeDtypeStruct((T, D), BF16),
            jax.ShapeDtypeStruct((T, D), BF16),
            jax.ShapeDtypeStruct((5, S), F32),
            jax.ShapeDtypeStruct((D, H), BF16),
            jax.ShapeDtypeStruct((H, D), BF16),
        ),
        in_specs=[any_space] * 5,
        out_specs=[any_space] * 5,
        scratch_shapes=[
            pltpu.VMEM((T, D), BF16),
            pltpu.VMEM((D, S), BF16),
            pltpu.VMEM((D, H), BF16),
            pltpu.VMEM((H, D), BF16),
            pltpu.VMEM((T, D), BF16),
            pltpu.VMEM((T, D), BF16),
            pltpu.VMEM((T, D), BF16),
            pltpu.VMEM((5, S), F32),
            pltpu.VMEM((D, H), BF16),
            pltpu.VMEM((H, D), BF16),
            pltpu.VMEM((4, SEQ, 16, H), BF16),
            pltpu.VMEM((4, SEQ, 16, H), BF16),
            pltpu.VMEM((4, XS, 2, D), F32),
            pltpu.VMEM((4, XS, 2, D), F32),
            pltpu.VMEM((4, SEQ, 16, H), BF16),
            pltpu.VMEM((8, 128), F32),
            pltpu.VMEM((SEQ, 8, 128), F32),
            pltpu.VMEM((8, 128), F32),
            pltpu.VMEM((SEQ, 8, 128), F32),
            pltpu.VMEM((SEQ, 80, 128), F32),
            pltpu.VMEM((SEQ, 80, 128), F32),
            pltpu.VMEM((88, 128), F32),
            pltpu.VMEM((16, 8, 128), F32),
            pltpu.VMEM((EXP, 8, 128), F32),
            dma((5,)), dma((5,)), dma((4,)), dma((4,)), dma((4,)), dma((4,)), dma((4,)), dma((4,)),
            dma((2,)), dma((2,)), dma((2,)), dma((2,)),
        ],
        compiler_params=pltpu.CompilerParams(
            collective_id=0, has_side_effects=True, vmem_limit_bytes=48 * 1024 * 1024
        ),
    )(tokens[0], router, w_in[0], w_out[0], grad_out[0])
    return mixed[None], d_tokens[None], d_router, d_w_in[None], d_w_out[None]


def solution(mesh):
    in_specs = (
        P("exp", "seq", None),
        P(),
        P("exp", None, "seq"),
        P("exp", "seq", None),
        P("exp", "seq", None),
    )
    out_specs = (
        P("exp", "seq", None),
        P("exp", "seq", None),
        P(("seq", "exp"), None),
        P("exp", None, "seq"),
        P("exp", "seq", None),
    )
    return jax.shard_map(shards, mesh=mesh, in_specs=in_specs, out_specs=out_specs, check_vma=False)
```

```python
import math

import jax
import jax.numpy as jnp
from jax import lax
from jax.experimental import pallas as pl
from jax.experimental.pallas import tpu as pltpu
from jax.sharding import PartitionSpec as P

F32 = jnp.float32
BF16 = jnp.bfloat16
MESH = pl.DeviceIdType.MESH
SEQ = 8
YS = 4
XS = 4
ZS = 8
D = 1280
H = 640
T = 512
S = 64
VMEM = 52 * 1024 * 1024


def nn(a, b):
    return lax.dot_general(a, b, (((1,), (0,)), ((), ())), preferred_element_type=F32)


def nt(a, b):
    return lax.dot_general(a, b, (((1,), (1,)), ((), ())), preferred_element_type=F32)


def split(a):
    high = a.astype(BF16)
    return high, (a - high.astype(F32)).astype(BF16)


def block(a, g):
    rows = a[8 * g : 8 * g + 8]
    return jnp.concatenate([rows[:, :H], rows[:, H:]], axis=0)


def store_blocks(ref, a):
    for g in range(SEQ):
        ref[g % 2, g // 2] = block(a, g).astype(ref.dtype)


def load_blocks(ref):
    parts = [ref[g % 2, g // 2].astype(F32) for g in range(SEQ)]
    lo = jnp.concatenate([p[:8, :H] for p in parts], axis=0)
    hi = jnp.concatenate([p[8:, :H] for p in parts], axis=0)
    return jnp.concatenate([lo, hi], axis=1).astype(BF16)


def pair_rows(top, low):
    square = jnp.concatenate(
        [jnp.broadcast_to(top, (S, 128)), jnp.broadcast_to(low, (S, 128))], axis=0
    )
    return square.T[:8]


def columns(rows):
    return jnp.concatenate([rows] * 16, axis=0).T


def left(a, b):
    lane = lax.broadcasted_iota(jnp.int32, a.shape, 1)
    return jnp.where(lane < S, a, pltpu.roll(b, S, 1))


def merge(stats):
    lane = lax.broadcasted_iota(jnp.int32, (8, 128), 1)
    top = stats[0]
    for s in stats[1:]:
        top = jnp.maximum(top, s)
    total = jnp.zeros((8, 128), F32)
    weights = []
    for s in stats:
        w = jnp.exp(jnp.where(lane < S, s - top, 0.0))
        weights.append(w)
        total = total + pltpu.roll(s, S, 1) * w
    return jnp.where(lane < S, top, 0.0), total, weights


def kernel(
    tokens_hbm, router_hbm, w_in_hbm, w_out_hbm, grad_hbm,
    mixed_v, d_tok_v, d_rout_v, d_w_in_v, d_w_out_v,
    tok, rout, w_in, w_out, grad,
    rc0, rc1, rc2, rc3, rm0, rm1, rm2, rm3, ry0, ry1, ry2, ry3, rr0, rr1, rr2, rr3,
    es0, es1, es2, es3, er0, er1, er2, er3, ag0, ag1, ag2, ag3,
    st_send, st_mid, st_core, st_recv, weight,
    tc_send, tc_mid, tc_sum, ty_send, ty_recv, ty_sum, tz_send, tz_recv,
    in_sem, send_sem, recv_sem,
):
    rc, rm, ry, rr = (rc0, rc1, rc2, rc3), (rm0, rm1, rm2, rm3), (ry0, ry1, ry2, ry3), (rr0, rr1, rr2, rr3)
    es, er, ag = (es0, es1, es2, es3), (er0, er1, er2, er3), (ag0, ag1, ag2, ag3)
    me_s = lax.axis_index("seq")
    me_n = lax.axis_index("exp")
    y = me_s // 2
    core = lax.rem(me_s, 2)
    z = me_n // XS
    x = lax.rem(me_n, XS)
    twin = me_s + 1 - 2 * core
    partner = lax.rem(me_s - z + SEQ, SEQ)
    own = lax.rem(core + z, 2)
    away = 1 - own
    mine = partner // 2

    loads = [
        pltpu.make_async_copy(src, dst, in_sem.at[i])
        for i, (src, dst) in enumerate(
            ((router_hbm, rout), (tokens_hbm, tok), (grad_hbm, grad), (w_in_hbm, w_in), (w_out_hbm, w_out))
        )
    ]
    loads[0].start()
    loads[1].start()

    barrier = pltpu.get_barrier_semaphore()

    def greet(s, n):
        pl.semaphore_signal(barrier, inc=1, device_id=(s, n), device_id_type=MESH)

    def ex_peer(k):
        return XS * partner + k

    for k in range(XS):

        @pl.when(ex_peer(k) != me_n)
        def _():
            greet(me_s, ex_peer(k))

    def greet_z(k, carry):
        greet(me_s, XS * lax.rem(z + k, ZS) + x)
        return carry

    def yx_peer(k):
        return 2 * lax.rem(y + k // XS, YS) + core, XS * z + lax.rem(x + lax.rem(k, XS), XS)

    def greet_yx(k, carry):
        greet(*yx_peer(k))
        return carry

    lax.fori_loop(1, ZS, greet_z, 0)
    lax.fori_loop(1, YS * XS, greet_yx, 0)
    greet(twin, me_n)

    def send(src, dst, sem, s, n):
        pltpu.make_async_remote_copy(
            src_ref=src, dst_ref=dst, send_sem=send_sem.at[sem], recv_sem=recv_sem.at[sem],
            device_id=(s, n), device_id_type=MESH,
        ).start()

    def all_of(ref, sem):
        pltpu.make_async_copy(ref, ref, sem).wait()

    def arrived(ref, sem):
        all_of(ref, recv_sem.at[sem])

    def over_y(make):
        def step(k, carry):
            make(2 * lax.rem(y + k, YS) + core)
            return carry

        lax.fori_loop(1, YS, step, 0)

    def rs_core(i):
        send(rc[i].at[away], rm[i], 5 * i, twin, me_n)

    def rs_y_send(i):
        rr[i][y] = ry[i][mine]
        over_y(
            lambda s: send(
                ry[i].at[lax.rem(s - z + SEQ, SEQ) // 2], rr[i].at[y], 5 * i + 1, s, me_n
            )
        )

    def rs_y(i):
        arrived(rm[i], 5 * i)
        for k in range(YS):
            ry[i][k] = (rc[i][own, k].astype(F32) + rm[i][k].astype(F32)).astype(ry[i].dtype)
        rs_y_send(i)

    def rs_total(i):
        arrived(rr[i].at[pl.ds(0, YS - 1)], 5 * i + 1)
        total = rr[i][0].astype(F32)
        for k in range(1, YS):
            total = total + rr[i][k].astype(F32)
        return total

    def ex_start(i, total, extra=None):
        rows = [total[:8], total[8:]]
        if extra is not None:
            rows.append(extra)
        rows = jnp.concatenate(rows, axis=1)
        for k in range(XS):
            es[i][k] = rows[2 * k : 2 * k + 2]
        for k in range(XS):

            @pl.when(ex_peer(k) != me_n)
            def _():
                send(es[i].at[k], er[i].at[x], 5 * i + 2, me_s, ex_peer(k))

            @pl.when(ex_peer(k) == me_n)
            def _():
                er[i][x] = es[i][k]

    def ex_rows(i):
        @pl.when(partner != z)
        def _():
            arrived(er[i], 5 * i + 2)

        @pl.when(partner == z)
        def _():
            arrived(er[i].at[pl.ds(0, XS - 1)], 5 * i + 2)

        return jnp.concatenate([er[i][k] for k in range(XS)], axis=0)

    def ag_start(i, rows):
        piece = jnp.concatenate([rows[:, :H], rows[:, H:D]], axis=0)
        if rows.shape[1] > D:
            value = rows[:, D:]
            high, rest = split(value)
            middle, low = split(value - high.astype(F32))
            lane = lax.broadcasted_iota(jnp.int32, (8, 128), 1)
            value = jnp.where(
                lane == 0,
                high.astype(F32),
                jnp.where(lane == 1, middle.astype(F32), jnp.where(lane == 2, low.astype(F32), 0.0)),
            )
            piece = jnp.concatenate(
                [piece, jnp.concatenate([value, jnp.zeros((8, 128), F32)], axis=0)], axis=1
            )
        ag[i][own, mine] = piece.astype(BF16)
        over_y(lambda s: send(ag[i].at[own, mine], ag[i].at[own, mine], 5 * i + 3, s, me_n))

    def ag_core(i):
        arrived(ag[i].at[0, pl.ds(0, YS - 1)], 5 * i + 3)
        send(ag[i].at[own], ag[i].at[own], 5 * i + 4, twin, me_n)

    def ag_finish(i):
        arrived(ag[i].at[0], 5 * i + 4)
        return load_blocks(ag[i])

    loads[0].wait()
    loads[1].wait()
    for load in loads[2:]:
        load.start()
    router_t = rout[...]
    logits = nt(router_t, tok[...])
    own_top = jnp.max(logits, axis=1, keepdims=True)
    own_exp = jnp.exp(logits - own_top)
    st_send[...] = pair_rows(own_top, jnp.sum(own_exp, axis=1, keepdims=True))
    exp_high, exp_low = split(own_exp)
    store_blocks(rc[1], nn(exp_high, tok[...]) + nn(exp_low, tok[...]))

    @pl.when(partner != z)
    def _():
        pl.semaphore_wait(barrier, 1 + YS * XS - 1 + ZS - 1 + XS)

    @pl.when(partner == z)
    def _():
        pl.semaphore_wait(barrier, 1 + YS * XS - 1 + ZS - 1 + XS - 1)

    rs_core(1)
    send(st_send, st_mid, 20, twin, me_n)
    row_exp = jnp.exp(logits - jnp.max(logits, axis=0, keepdims=True))
    combine = row_exp / jnp.sum(row_exp, axis=0, keepdims=True)
    loads[2].wait()
    store_blocks(rc[0], nn(combine.astype(BF16), grad[...]))
    rs_core(0)

    arrived(st_mid, 20)
    top, total, (w_own, w_mid) = merge([st_send[...], st_mid[...]])
    st_core[...] = left(top, total)
    weight[...] = columns(left(w_own, w_mid))
    arrived(rm[1], 5)
    for k in range(YS):
        g = pl.multiple_of(8 * (own + 2 * k), 8)
        a = weight[pl.ds(g, 8)]
        b = weight[pl.ds(S + g, 8)]
        a = jnp.concatenate([jnp.concatenate([a] * 5, axis=1)] * 2, axis=0)
        b = jnp.concatenate([jnp.concatenate([b] * 5, axis=1)] * 2, axis=0)
        ry[1][k] = rc[1][own, k] * a + rm[1][k] * b
    st_recv[y] = st_core[...]
    over_y(lambda s: send(st_core, st_recv.at[y], 21, s, me_n))
    rs_y_send(1)
    rs_y(0)

    arrived(st_recv.at[pl.ds(0, YS - 1)], 21)
    stats = [st_recv[k] for k in range(YS)]
    top, total, ws = merge(stats)
    w = [v / total for v in ws]
    weight[...] = columns(left(w[0], w[1]))
    g = pl.multiple_of(8 * partner, 8)
    w0, w1 = weight[pl.ds(g, 8)], weight[pl.ds(S + g, 8)]
    weight[...] = columns(left(w[2], w[3]))
    w2, w3 = weight[pl.ds(g, 8)], weight[pl.ds(S + g, 8)]
    arrived(rr[1].at[pl.ds(0, YS - 1)], 6)
    total_in = jnp.zeros((16, H), F32)
    for k, v in enumerate((w0, w1, w2, w3)):
        total_in = total_in + rr[1][k] * jnp.concatenate([jnp.concatenate([v] * 5, axis=1)] * 2, axis=0)
    ex_start(1, total_in)
    ex_start(0, rs_total(0))
    scale = columns(left(jnp.exp(st_send[...] - top) / total, total))[:S, :1]
    dispatch = own_exp * scale

    rows_1 = ex_rows(1)
    ag_start(1, rows_1)
    ag_start(0, ex_rows(0))
    ag_core(1)
    ag_core(0)

    loads[3].wait()
    rows = ag_finish(1)
    hidden = nn(rows, w_in[...])
    cdf = 0.5 * (1.0 + lax.erf(hidden * (1.0 / math.sqrt(2.0))))
    act = hidden * cdf
    loads[4].wait()
    store_blocks(rc[3], nn(act.astype(BF16), w_out[...]))
    rs_core(3)
    pdf = jnp.exp(-0.5 * hidden * hidden) * (1.0 / math.sqrt(2.0 * math.pi))
    slope = cdf + hidden * pdf
    d_rows = ag_finish(0)
    d_hidden_b = (nt(d_rows, w_out[...]) * slope).astype(BF16)
    store_blocks(rc[2], nt(d_hidden_b, w_in[...]))
    rs_core(2)

    rs_y(3)
    rs_y(2)
    act_t = act.T.astype(BF16)
    for k in range(5):
        part = slice(128 * k, 128 * k + 128)
        d_w_out_v[part] = nn(act_t[part], d_rows).astype(BF16)
    ex_start(3, rs_total(3))
    total = rs_total(2).astype(BF16).astype(F32)
    column = jnp.sum(total[:8] * rows_1[:, :H] + total[8:] * rows_1[:, H:], axis=1, keepdims=True)
    ex_start(2, total, jnp.broadcast_to(column, (8, 128)))
    rows_t = rows.astype(F32).T.astype(BF16)
    for k in range(10):
        part = slice(128 * k, 128 * k + 128)
        d_w_in_v[part] = nn(rows_t[part], d_hidden_b).astype(BF16)
    ag_start(3, ex_rows(3))
    ag_start(2, ex_rows(2))
    ag_core(3)
    ag_core(2)

    slots_out = ag_finish(3)
    d_combine = nt(slots_out, grad[...])
    d_logit_c = combine * (d_combine - jnp.sum(combine * d_combine, axis=0, keepdims=True))
    d_slots = ag_finish(2)
    column = jnp.concatenate(
        [ag[2][g % 2, g // 2, :8, H:].astype(F32) for g in range(SEQ)], axis=0
    )
    column = jnp.sum(column, axis=1, keepdims=True)
    d_dispatch = nt(d_slots, tok[...])
    d_logit = d_logit_c + dispatch * (d_dispatch - column)

    d_router_t = nn(d_logit.astype(BF16), tok[...])
    pair = jnp.concatenate([d_router_t, pltpu.roll(d_router_t, D - 80, 1)], axis=0).T
    for k in range(SEQ):
        tc_send[k % 2, k // 2] = pair[160 * k : 160 * k + 80]
    send(tc_send.at[1 - core], tc_mid, 22, twin, me_n)
    combine_t = combine.T.astype(BF16)
    for k in range(4):
        part = slice(128 * k, 128 * k + 128)
        mixed_v[part] = nn(combine_t[part], slots_out).astype(BF16)
    arrived(tc_mid, 22)
    for k in range(YS):
        tc_sum[k] = tc_send[core, k] + tc_mid[k]
    for k in range(YS):
        for j in range(XS):
            for i in range(4):
                ty_send[k, j, 5 * i : 5 * i + 5] = tc_sum[k, 20 * i + 5 * j : 20 * i + 5 * j + 5]
    ty_recv[XS * y + x] = ty_send[y, x]

    def send_yx(k, carry):
        s, n = yx_peer(k)
        send(ty_send.at[s // 2, lax.rem(n, XS)], ty_recv.at[XS * y + x], 23, s, n)
        return carry

    lax.fori_loop(1, YS * XS, send_yx, 0)
    weights = jnp.concatenate([dispatch, d_logit], axis=0).T.astype(BF16)
    values = jnp.concatenate([d_slots, router_t], axis=0)
    for k in range(4):
        part = slice(128 * k, 128 * k + 128)
        d_tok_v[part] = nn(weights[part], values).astype(BF16)
    arrived(ty_recv.at[pl.ds(0, YS * XS - 1)], 23)
    total = ty_recv[0]
    for k in range(1, YS * XS):
        total = total + ty_recv[k]
    ty_sum[...] = total
    for k in range(4):
        tz_send[k] = ty_sum[5 * k : 5 * k + 8]
    tz_recv[z] = tz_send[lax.rem(z, 4)]

    def send_z(k, carry):
        to = lax.rem(z + k, ZS)
        send(tz_send.at[lax.rem(to, 4)], tz_recv.at[z], 24, me_s, XS * to + x)
        return carry

    lax.fori_loop(1, ZS, send_z, 0)
    arrived(tz_recv.at[pl.ds(0, ZS - 1)], 24)
    total = tz_recv[0]
    for k in range(1, ZS):
        total = total + tz_recv[k]
    total = jnp.where(z >= 4, pltpu.roll(total, S, 1), total)
    d_rout_v[...] = total[:5, :S]

    for i in range(4):
        all_of(rm[i], send_sem.at[5 * i])
        all_of(rr[i].at[pl.ds(0, YS - 1)], send_sem.at[5 * i + 1])

        @pl.when(partner != z)
        def _():
            all_of(er[i], send_sem.at[5 * i + 2])

        @pl.when(partner == z)
        def _():
            all_of(er[i].at[pl.ds(0, XS - 1)], send_sem.at[5 * i + 2])

        all_of(ag[i].at[0, pl.ds(0, YS - 1)], send_sem.at[5 * i + 3])
        all_of(ag[i].at[0], send_sem.at[5 * i + 4])
    all_of(st_mid, send_sem.at[20])
    all_of(st_recv.at[pl.ds(0, YS - 1)], send_sem.at[21])
    all_of(tc_mid, send_sem.at[22])
    all_of(ty_recv.at[pl.ds(0, YS * XS - 1)], send_sem.at[23])
    all_of(tz_recv.at[pl.ds(0, ZS - 1)], send_sem.at[24])


def store(a0, a1, a2, a3, a4, b0, b1, b2, b3, b4, sem):
    copies = [
        pltpu.make_async_copy(a, b, sem.at[i])
        for i, (a, b) in enumerate(((a0, b0), (a1, b1), (a2, b2), (a3, b3), (a4, b4)))
    ]
    for copy in copies:
        copy.start()
    for copy in copies:
        copy.wait()


def shards(tokens, router, w_in, w_out, grad_out):
    any_space = pl.BlockSpec(memory_space=pl.ANY)
    dma = pltpu.SemaphoreType.DMA
    vmem = pltpu.VMEM
    kinds = (BF16, F32, BF16, BF16)
    wide = (0, 0, 128, 0)
    results = pl.pallas_call(
        kernel,
        out_shape=(
            vmem((T, D), BF16),
            vmem((T, D), BF16),
            vmem((5, S), F32),
            vmem((D, H), BF16),
            vmem((H, D), BF16),
        ),
        in_specs=[any_space] * 5,
        out_specs=[pl.BlockSpec(memory_space=vmem)] * 5,
        scratch_shapes=[
            vmem((T, D), BF16),
            vmem((S, D), BF16),
            vmem((D, H), BF16),
            vmem((H, D), BF16),
            vmem((T, D), BF16),
            *[vmem((2, 4, 16, H), k) for k in kinds],
            *[vmem((4, 16, H), k) for k in kinds],
            *[vmem((4, 16, H), k) for k in kinds],
            *[vmem((4, 16, H), k) for k in kinds],
            *[vmem((XS, 2, D + w), F32) for w in wide],
            *[vmem((XS, 2, D + w), F32) for w in wide],
            *[vmem((2, 4, 16, H + w), BF16) for w in wide],
            vmem((8, 128), F32),
            vmem((8, 128), F32),
            vmem((8, 128), F32),
            vmem((YS, 8, 128), F32),
            vmem((128, 128), F32),
            vmem((2, YS, 80, 128), F32),
            vmem((YS, 80, 128), F32),
            vmem((YS, 80, 128), F32),
            vmem((YS, XS, 24, 128), F32),
            vmem((YS * XS, 24, 128), F32),
            vmem((24, 128), F32),
            vmem((4, 8, 128), F32),
            vmem((ZS, 8, 128), F32),
            dma((5,)), dma((25,)), dma((25,)),
        ],
        compiler_params=pltpu.CompilerParams(
            collective_id=0, has_side_effects=True, vmem_limit_bytes=VMEM
        ),
    )(tokens[0], router.T, w_in[0], w_out[0], grad_out[0])
    mixed, d_tokens, d_router, d_w_in, d_w_out = pl.pallas_call(
        store,
        out_shape=tuple(jax.ShapeDtypeStruct(r.shape, r.dtype) for r in results),
        in_specs=[pl.BlockSpec(memory_space=vmem)] * 5,
        out_specs=[any_space] * 5,
        scratch_shapes=[dma((5,))],
        compiler_params=pltpu.CompilerParams(vmem_limit_bytes=4 * 1024 * 1024),
    )(*results)
    return mixed[None], d_tokens[None], d_router, d_w_in[None], d_w_out[None]


def solution(mesh):
    in_specs = (
        P("exp", "seq", None),
        P(),
        P("exp", None, "seq"),
        P("exp", "seq", None),
        P("exp", "seq", None),
    )
    out_specs = (
        P("exp", "seq", None),
        P("exp", "seq", None),
        P(("seq", "exp"), None),
        P("exp", None, "seq"),
        P("exp", "seq", None),
    )
    return jax.shard_map(shards, mesh=mesh, in_specs=in_specs, out_specs=out_specs, check_vma=False)
```

```python
import math

import jax
import jax.numpy as jnp
from jax import lax
from jax.experimental import pallas as pl
from jax.experimental.pallas import tpu as pltpu
from jax.sharding import PartitionSpec as P

F32 = jnp.float32
BF16 = jnp.bfloat16
MESH = pl.DeviceIdType.MESH
SEQ = 8
YS = 4
XS = 4
ZS = 8
DIRECT = (0, 2)
NEAR = (1, 2, ZS - 2, ZS - 1)
D = 1280
H = 640
T = 512
S = 64
VMEM = 52 * 1024 * 1024


def nn(a, b):
    return lax.dot_general(a, b, (((1,), (0,)), ((), ())), preferred_element_type=F32)


def nt(a, b):
    return lax.dot_general(a, b, (((1,), (1,)), ((), ())), preferred_element_type=F32)


def split(a):
    high = a.astype(BF16)
    return high, (a - high.astype(F32)).astype(BF16)


def thirds(column):
    value = jnp.broadcast_to(column, (8, 128))
    high, rest = split(value)
    middle, low = split(value - high.astype(F32))
    lane = lax.broadcasted_iota(jnp.int32, (8, 128), 1)
    value = jnp.where(lane == 2, low.astype(F32), 0.0)
    value = jnp.where(lane == 1, middle.astype(F32), value)
    return jnp.where(lane == 0, high.astype(F32), value)


def block(a, g):
    rows = a[8 * g : 8 * g + 8]
    return jnp.concatenate([rows[:, :H], rows[:, H:]], axis=0)


def store_blocks(ref, a):
    for g in range(SEQ):
        ref[g % 2, g // 2] = block(a, g).astype(ref.dtype)


def load_blocks(ref):
    parts = [ref[4 * (g % 2) + g // 2].astype(F32) for g in range(SEQ)]
    lo = jnp.concatenate([p[:8, :H] for p in parts], axis=0)
    hi = jnp.concatenate([p[8:, :H] for p in parts], axis=0)
    return jnp.concatenate([lo, hi], axis=1).astype(BF16)


def pair_rows(top, low):
    square = jnp.concatenate(
        [jnp.broadcast_to(top, (S, 128)), jnp.broadcast_to(low, (S, 128))], axis=0
    )
    return square.T[:8]


def columns(rows):
    return jnp.concatenate([rows] * 16, axis=0).T


def left(a, b):
    lane = lax.broadcasted_iota(jnp.int32, a.shape, 1)
    return jnp.where(lane < S, a, pltpu.roll(b, S, 1))


def merge(stats):
    lane = lax.broadcasted_iota(jnp.int32, (8, 128), 1)
    top = stats[0]
    for s in stats[1:]:
        top = jnp.maximum(top, s)
    total = jnp.zeros((8, 128), F32)
    weights = []
    for s in stats:
        w = jnp.exp(jnp.where(lane < S, s - top, 0.0))
        weights.append(w)
        total = total + pltpu.roll(s, S, 1) * w
    return jnp.where(lane < S, top, 0.0), total, weights


def kernel(
    tokens_hbm, router_hbm, w_in_hbm, w_out_hbm, grad_hbm,
    mixed_v, d_tok_v, d_rout_v, d_w_in_v, d_w_out_v,
    tok, rout, w_in, w_out, grad,
    rc0, rc1, rc2, rc3, rm0, rm1, rm2, rm3, ry0, ry1, ry2, ry3, rr0, rr1, rr2, rr3,
    es0, es1, es2, es3, er0, er1, er2, er3, ag0, ag1, ag2, ag3,
    st_send, st_mid, st_core, st_recv, weight,
    tc_send, tc_mid, tc_sum, ty_send, ty_recv, tz_send, tz_recv,
    in_sem, send_sem, recv_sem, hello,
):
    rc, rm, ry, rr = (rc0, rc1, rc2, rc3), (rm0, rm1, rm2, rm3), (ry0, ry1, ry2, ry3), (rr0, rr1, rr2, rr3)
    es, er, ag = (es0, es1, es2, es3), (er0, er1, er2, er3), (ag0, ag1, ag2, ag3)
    me_s = lax.axis_index("seq")
    me_n = lax.axis_index("exp")
    y = me_s // 2
    core = lax.rem(me_s, 2)
    z = me_n // XS
    x = lax.rem(me_n, XS)
    twin = me_s + 1 - 2 * core
    partner = lax.rem(me_s - z + SEQ, SEQ)
    own = lax.rem(core + z, 2)
    away = 1 - own
    mine = partner // 2

    loads = [
        pltpu.make_async_copy(src, dst, in_sem.at[i])
        for i, (src, dst) in enumerate(
            ((router_hbm, rout), (grad_hbm, grad), (w_in_hbm, w_in), (w_out_hbm, w_out))
        )
    ]
    pieces = [
        pltpu.make_async_copy(
            tokens_hbm.at[pl.ds(128 * k, 128)], tok.at[pl.ds(128 * k, 128)], in_sem.at[4 + k]
        )
        for k in range(4)
    ]
    loads[0].start()
    for piece in pieces:
        piece.start()

    barrier = pltpu.get_barrier_semaphore()

    def greet(s, n):
        pl.semaphore_signal(barrier, inc=1, device_id=(s, n), device_id_type=MESH)

    def ex_peer(k):
        return XS * partner + k

    def yx_peer(k):
        return 2 * lax.rem(y + k // XS, YS) + core, XS * z + lax.rem(x + lax.rem(k, XS), XS)

    along_x = [XS * z + lax.rem(x + k, XS) for k in range(1, XS)]
    along_z = [XS * lax.rem(z + k, ZS) + x for k in NEAR]
    for k in range(1, YS):
        greet(2 * lax.rem(y + k, YS) + core, me_n)
    for n in along_x + along_z:
        greet(me_s, n)
    greet(twin, me_n)

    def pass_on(sem, devices):
        for n in devices:
            pl.semaphore_signal(
                hello.at[sem], inc=1, device_id=(me_s, n), device_id_type=MESH
            )

    def send(src, dst, sem, s, n):
        pltpu.make_async_remote_copy(
            src_ref=src, dst_ref=dst, send_sem=send_sem.at[sem], recv_sem=recv_sem.at[sem],
            device_id=(s, n), device_id_type=MESH,
        ).start()

    def all_of(ref, sem):
        pltpu.make_async_copy(ref, ref, sem).wait()

    def arrived(ref, sem):
        all_of(ref, recv_sem.at[sem])

    def over_y(make):
        def step(k, carry):
            make(2 * lax.rem(y + k, YS) + core)
            return carry

        lax.fori_loop(1, YS, step, 0)

    def rs_core(i):
        send(rc[i].at[away], rm[i], 5 * i, twin, me_n)

    def rs_y_send(i):
        rr[i][y] = ry[i][mine]
        over_y(
            lambda s: send(
                ry[i].at[lax.rem(s - z + SEQ, SEQ) // 2], rr[i].at[y], 5 * i + 1, s, me_n
            )
        )

    def rs_y(i):
        arrived(rm[i], 5 * i)
        for k in range(YS):
            ry[i][k] = (rc[i][own, k].astype(F32) + rm[i][k].astype(F32)).astype(ry[i].dtype)
        rs_y_send(i)

    def rs_total(i):
        arrived(rr[i].at[pl.ds(0, YS - 1)], 5 * i + 1)
        total = rr[i][0].astype(F32)
        for k in range(1, YS):
            total = total + rr[i][k].astype(F32)
        return total

    def ex_start(i, total, extra=None):
        rows = [total[:8], total[8:]]
        if extra is not None:
            rows.append(extra)
        rows = jnp.concatenate(rows, axis=1)
        for k in range(XS):
            es[i][k] = rows[2 * k : 2 * k + 2].astype(es[i].dtype)
        for k in range(XS):

            @pl.when(ex_peer(k) != me_n)
            def _():
                send(es[i].at[k], er[i].at[x], 5 * i + 2, me_s, ex_peer(k))

            @pl.when(ex_peer(k) == me_n)
            def _():
                er[i][x] = es[i][k]

    def ex_rows(i):
        @pl.when(partner != z)
        def _():
            arrived(er[i], 5 * i + 2)

        @pl.when(partner == z)
        def _():
            arrived(er[i].at[pl.ds(0, XS - 1)], 5 * i + 2)

        return jnp.concatenate([er[i][k].astype(F32) for k in range(XS)], axis=0)

    def ag_start(i, rows):
        piece = jnp.concatenate([rows[:, :H], rows[:, H:D]], axis=0)
        if rows.shape[1] > D:
            extra = jnp.concatenate([rows[:, D:], jnp.zeros((8, 128), F32)], axis=0)
            piece = jnp.concatenate([piece, extra], axis=1)
        ag[i][4 * own + mine] = piece.astype(BF16)
        if i in DIRECT:
            for k in range(1, SEQ):
                send(
                    ag[i].at[4 * own + mine], ag[i].at[4 * own + mine], 5 * i + 3, lax.rem(me_s + k, SEQ), me_n
                )
        else:
            over_y(lambda s: send(ag[i].at[4 * own + mine], ag[i].at[4 * own + mine], 5 * i + 3, s, me_n))

    def ag_core(i):
        if i in DIRECT:
            return
        arrived(ag[i].at[pl.ds(0, YS - 1)], 5 * i + 3)
        half = ag[i].at[pl.ds(pl.multiple_of(4 * own, 4), 4)]
        send(half, half, 5 * i + 4, twin, me_n)

    def ag_finish(i):
        if i in DIRECT:
            arrived(ag[i].at[pl.ds(0, SEQ - 1)], 5 * i + 3)
        else:
            arrived(ag[i].at[pl.ds(0, YS)], 5 * i + 4)
        return load_blocks(ag[i])

    loads[0].wait()
    for piece in pieces:
        piece.wait()
    for load in loads[1:]:
        load.start()
    router_t = rout[...]
    logits = nt(router_t, tok[...])
    own_top = jnp.max(logits, axis=1, keepdims=True)
    own_exp = jnp.exp(logits - own_top)
    st_send[...] = pair_rows(own_top, jnp.sum(own_exp, axis=1, keepdims=True))
    exp_high, exp_low = split(own_exp)
    store_blocks(rc[1], nn(exp_high, tok[...]) + nn(exp_low, tok[...]))

    pl.semaphore_wait(barrier, 1 + YS - 1 + XS - 1 + len(NEAR))
    rs_core(1)
    send(st_send, st_mid, 20, twin, me_n)
    pass_on(0, along_x + along_z)
    row_exp = jnp.exp(logits - jnp.max(logits, axis=0, keepdims=True))
    combine = row_exp / jnp.sum(row_exp, axis=0, keepdims=True)
    loads[1].wait()
    store_blocks(rc[0], nn(combine.astype(BF16), grad[...]))
    rs_core(0)

    arrived(st_mid, 20)
    top, total, (w_own, w_mid) = merge([st_send[...], st_mid[...]])
    st_core[...] = left(top, total)
    weight[...] = columns(left(w_own, w_mid))
    arrived(rm[1], 5)
    for k in range(YS):
        g = pl.multiple_of(8 * (own + 2 * k), 8)
        a = weight[pl.ds(g, 8)]
        b = weight[pl.ds(S + g, 8)]
        a = jnp.concatenate([jnp.concatenate([a] * 5, axis=1)] * 2, axis=0)
        b = jnp.concatenate([jnp.concatenate([b] * 5, axis=1)] * 2, axis=0)
        ry[1][k] = rc[1][own, k] * a + rm[1][k] * b
    st_recv[y] = st_core[...]
    over_y(lambda s: send(st_core, st_recv.at[y], 21, s, me_n))
    rs_y_send(1)
    rs_y(0)
    pl.semaphore_wait(hello.at[0], XS - 1 + len(NEAR))
    pass_on(1, along_z)

    arrived(st_recv.at[pl.ds(0, YS - 1)], 21)
    stats = [st_recv[k] for k in range(YS)]
    top, total, ws = merge(stats)
    w = [v / total for v in ws]
    weight[...] = columns(left(w[0], w[1]))
    g = pl.multiple_of(8 * partner, 8)
    w0, w1 = weight[pl.ds(g, 8)], weight[pl.ds(S + g, 8)]
    weight[...] = columns(left(w[2], w[3]))
    w2, w3 = weight[pl.ds(g, 8)], weight[pl.ds(S + g, 8)]
    arrived(rr[1].at[pl.ds(0, YS - 1)], 6)
    total_in = jnp.zeros((16, H), F32)
    for k, v in enumerate((w0, w1, w2, w3)):
        total_in = total_in + rr[1][k] * jnp.concatenate([jnp.concatenate([v] * 5, axis=1)] * 2, axis=0)
    pl.semaphore_wait(hello.at[1], len(NEAR))
    ex_start(1, total_in)
    ex_start(0, rs_total(0))
    scale = columns(left(jnp.exp(st_send[...] - top) / total, total))[:S, :1]
    dispatch = own_exp * scale

    rows_1 = ex_rows(1)
    ag_start(1, rows_1)
    ag_start(0, ex_rows(0))
    ag_core(1)
    ag_core(0)

    loads[2].wait()
    rows = ag_finish(1)
    hidden = nn(rows, w_in[...])
    cdf = 0.5 * (1.0 + lax.erf(hidden * (1.0 / math.sqrt(2.0))))
    act = hidden * cdf
    loads[3].wait()
    store_blocks(rc[3], nn(act.astype(BF16), w_out[...]))
    rs_core(3)
    pdf = jnp.exp(-0.5 * hidden * hidden) * (1.0 / math.sqrt(2.0 * math.pi))
    slope = cdf + hidden * pdf
    d_rows = ag_finish(0)
    d_hidden_b = (nt(d_rows, w_out[...]) * slope).astype(BF16)
    store_blocks(rc[2], nt(d_hidden_b, w_in[...]))
    rs_core(2)

    rs_y(3)
    rs_y(2)
    act_t = act.T.astype(BF16)
    for k in range(5):
        part = slice(128 * k, 128 * k + 128)
        d_w_out_v[part] = nn(act_t[part], d_rows).astype(BF16)
    ex_start(3, rs_total(3))
    total = rs_total(2).astype(BF16).astype(F32)
    column = jnp.sum(total[:8] * rows_1[:, :H] + total[8:] * rows_1[:, H:], axis=1, keepdims=True)
    ex_start(2, total, thirds(column))
    rows_t = rows.astype(F32).T.astype(BF16)
    for k in range(10):
        part = slice(128 * k, 128 * k + 128)
        d_w_in_v[part] = nn(rows_t[part], d_hidden_b).astype(BF16)
    ag_start(3, ex_rows(3))
    ag_start(2, ex_rows(2))
    ag_core(3)
    ag_core(2)

    slots_out = ag_finish(3)
    d_combine = nt(slots_out, grad[...])
    d_logit_c = combine * (d_combine - jnp.sum(combine * d_combine, axis=0, keepdims=True))
    d_slots = ag_finish(2)
    column = jnp.concatenate(
        [ag[2][4 * (g % 2) + g // 2, :8, H:].astype(F32) for g in range(SEQ)], axis=0
    )
    column = jnp.sum(column, axis=1, keepdims=True)
    d_dispatch = nt(d_slots, tok[...])
    d_logit = d_logit_c + dispatch * (d_dispatch - column)

    d_router_t = nn(d_logit.astype(BF16), tok[...])
    pair = jnp.concatenate([d_router_t, pltpu.roll(d_router_t, D - 80, 1)], axis=0).T
    for k in range(SEQ):
        tc_send[k % 2, k // 2] = pair[160 * k : 160 * k + 80]
    send(tc_send.at[1 - core], tc_mid, 22, twin, me_n)
    combine_t = combine.T.astype(BF16)
    for k in range(4):
        part = slice(128 * k, 128 * k + 128)
        mixed_v[part] = nn(combine_t[part], slots_out).astype(BF16)
    arrived(tc_mid, 22)
    for k in range(YS):
        tc_sum[k] = tc_send[core, k] + tc_mid[k]
    for k in range(YS):
        for j in range(XS):
            for i in range(5):
                ty_send[k, j, i] = tc_sum[k, pl.ds(5 * j + i, 4, stride=20), :]
    ty_recv[XS * y + x] = ty_send[y, x]

    def send_yx(k, carry):
        s, n = yx_peer(k)
        send(ty_send.at[s // 2, lax.rem(n, XS)], ty_recv.at[XS * y + x], 23, s, n)
        return carry

    lax.fori_loop(1, YS * XS, send_yx, 0)
    weights = jnp.concatenate([dispatch, d_logit], axis=0).T.astype(BF16)
    values = jnp.concatenate([d_slots, router_t], axis=0)
    for k in range(4):
        part = slice(128 * k, 128 * k + 128)
        d_tok_v[part] = nn(weights[part], values).astype(BF16)
    arrived(ty_recv.at[pl.ds(0, YS * XS - 1)], 23)
    total = ty_recv[0]
    for k in range(1, YS * XS):
        total = total + ty_recv[k]
    tz_send[...] = jnp.zeros((ZS, 4, 128), F32)
    for k in range(3):
        first = total[2 * k]
        second = total[2 * k + 1] if k < 2 else jnp.zeros((4, 128), F32)
        for half, packed in enumerate((left(first, second), left(pltpu.roll(first, S, 1), pltpu.roll(second, S, 1)))):
            for i in range(4):
                tz_send[4 * half + i, k : k + 1] = packed[i : i + 1]
    tz_recv[z] = tz_send[z]

    def send_z(k, carry):
        to = lax.rem(z + k, ZS)
        send(tz_send.at[to], tz_recv.at[z], 24, me_s, XS * to + x)
        return carry

    lax.fori_loop(1, ZS, send_z, 0)
    arrived(tz_recv.at[pl.ds(0, ZS - 1)], 24)
    total = tz_recv[0]
    for k in range(1, ZS):
        total = total + tz_recv[k]
    other = pltpu.roll(total, S, 1)
    for k in range(5):
        d_rout_v[k : k + 1] = (other if k % 2 else total)[k // 2 : k // 2 + 1, :S]

    for i in range(4):
        all_of(rm[i], send_sem.at[5 * i])
        all_of(rr[i].at[pl.ds(0, YS - 1)], send_sem.at[5 * i + 1])

        @pl.when(partner != z)
        def _():
            all_of(er[i], send_sem.at[5 * i + 2])

        @pl.when(partner == z)
        def _():
            all_of(er[i].at[pl.ds(0, XS - 1)], send_sem.at[5 * i + 2])

        if i in DIRECT:
            all_of(ag[i].at[pl.ds(0, SEQ - 1)], send_sem.at[5 * i + 3])
        else:
            all_of(ag[i].at[pl.ds(0, YS - 1)], send_sem.at[5 * i + 3])
            all_of(ag[i].at[pl.ds(0, YS)], send_sem.at[5 * i + 4])
    all_of(st_mid, send_sem.at[20])
    all_of(st_recv.at[pl.ds(0, YS - 1)], send_sem.at[21])
    all_of(tc_mid, send_sem.at[22])
    all_of(ty_recv.at[pl.ds(0, YS * XS - 1)], send_sem.at[23])
    all_of(tz_recv.at[pl.ds(0, ZS - 1)], send_sem.at[24])


def store(a0, a1, a2, a3, a4, b0, b1, b2, b3, b4, sem):
    copies = [
        pltpu.make_async_copy(a, b, sem.at[i])
        for i, (a, b) in enumerate(((a0, b0), (a1, b1), (a2, b2), (a3, b3), (a4, b4)))
    ]
    for copy in copies:
        copy.start()
    for copy in copies:
        copy.wait()


def shards(tokens, router, w_in, w_out, grad_out):
    any_space = pl.BlockSpec(memory_space=pl.ANY)
    dma = pltpu.SemaphoreType.DMA
    vmem = pltpu.VMEM
    kinds = (BF16, F32, BF16, BF16)
    wide = (0, 0, 128, 0)
    results = pl.pallas_call(
        kernel,
        out_shape=(
            vmem((T, D), BF16),
            vmem((T, D), BF16),
            vmem((5, S), F32),
            vmem((D, H), BF16),
            vmem((H, D), BF16),
        ),
        in_specs=[any_space] * 5,
        out_specs=[pl.BlockSpec(memory_space=vmem)] * 5,
        scratch_shapes=[
            vmem((T, D), BF16),
            vmem((S, D), BF16),
            vmem((D, H), BF16),
            vmem((H, D), BF16),
            vmem((T, D), BF16),
            *[vmem((2, 4, 16, H), k) for k in kinds],
            *[vmem((4, 16, H), k) for k in kinds],
            *[vmem((4, 16, H), k) for k in kinds],
            *[vmem((4, 16, H), k) for k in kinds],
            *[vmem((XS, 2, D + w), k) for w, k in zip(wide, kinds)],
            *[vmem((XS, 2, D + w), k) for w, k in zip(wide, kinds)],
            *[vmem((SEQ, 16, H + w), BF16) for w in wide],
            vmem((8, 128), F32),
            vmem((8, 128), F32),
            vmem((8, 128), F32),
            vmem((YS, 8, 128), F32),
            vmem((128, 128), F32),
            vmem((2, YS, 80, 128), F32),
            vmem((YS, 80, 128), F32),
            vmem((YS, 80, 128), F32),
            vmem((YS, XS, 5, 4, 128), F32),
            vmem((YS * XS, 5, 4, 128), F32),
            vmem((ZS, 4, 128), F32),
            vmem((ZS, 4, 128), F32),
            dma((8,)), dma((25,)), dma((25,)), pltpu.SemaphoreType.REGULAR((2,)),
        ],
        compiler_params=pltpu.CompilerParams(
            collective_id=0, has_side_effects=True, vmem_limit_bytes=VMEM
        ),
    )(tokens[0], router.T, w_in[0], w_out[0], grad_out[0])
    mixed, d_tokens, d_router, d_w_in, d_w_out = pl.pallas_call(
        store,
        out_shape=tuple(jax.ShapeDtypeStruct(r.shape, r.dtype) for r in results),
        in_specs=[pl.BlockSpec(memory_space=vmem)] * 5,
        out_specs=[any_space] * 5,
        scratch_shapes=[dma((5,))],
        compiler_params=pltpu.CompilerParams(vmem_limit_bytes=4 * 1024 * 1024),
    )(*results)
    return mixed[None], d_tokens[None], d_router, d_w_in[None], d_w_out[None]


def solution(mesh):
    in_specs = (
        P("exp", "seq", None),
        P(),
        P("exp", None, "seq"),
        P("exp", "seq", None),
        P("exp", "seq", None),
    )
    out_specs = (
        P("exp", "seq", None),
        P("exp", "seq", None),
        P(("seq", "exp"), None),
        P("exp", None, "seq"),
        P("exp", "seq", None),
    )
    return jax.shard_map(shards, mesh=mesh, in_specs=in_specs, out_specs=out_specs, check_vma=False)
```

```python
import math

import jax
import jax.numpy as jnp
from jax import lax
from jax.experimental import pallas as pl
from jax.experimental.pallas import tpu as pltpu
from jax.sharding import PartitionSpec as P

F32 = jnp.float32
BF16 = jnp.bfloat16
MESH = pl.DeviceIdType.MESH
SEQ = 8
YS = 4
XS = 4
ZS = 8
DIRECT = (0, 1, 2)
NEAR = (1, 2, ZS - 2, ZS - 1)
D = 1280
H = 640
T = 512
S = 64
VMEM = 52 * 1024 * 1024


def nn(a, b):
    return lax.dot_general(a, b, (((1,), (0,)), ((), ())), preferred_element_type=F32)


def nt(a, b):
    return lax.dot_general(a, b, (((1,), (1,)), ((), ())), preferred_element_type=F32)


def split(a):
    high = a.astype(BF16)
    return high, (a - high.astype(F32)).astype(BF16)


def thirds(column):
    value = jnp.broadcast_to(column, (8, 128))
    high, rest = split(value)
    middle, low = split(value - high.astype(F32))
    lane = lax.broadcasted_iota(jnp.int32, (8, 128), 1)
    value = jnp.where(lane == 2, low.astype(F32), 0.0)
    value = jnp.where(lane == 1, middle.astype(F32), value)
    return jnp.where(lane == 0, high.astype(F32), value)


def block(a, g):
    rows = a[8 * g : 8 * g + 8]
    return jnp.concatenate([rows[:, :H], rows[:, H:]], axis=0)


def store_blocks(ref, a):
    for g in range(SEQ):
        ref[g % 2, g // 2] = block(a, g).astype(ref.dtype)


def load_blocks(ref):
    parts = [ref[4 * (g % 2) + g // 2].astype(F32) for g in range(SEQ)]
    lo = jnp.concatenate([p[:8, :H] for p in parts], axis=0)
    hi = jnp.concatenate([p[8:, :H] for p in parts], axis=0)
    return jnp.concatenate([lo, hi], axis=1).astype(BF16)


def pair_rows(top, low):
    square = jnp.concatenate(
        [jnp.broadcast_to(top, (S, 128)), jnp.broadcast_to(low, (S, 128))], axis=0
    )
    return square.T[:8]


def columns(rows):
    return jnp.concatenate([rows] * 16, axis=0).T


def left(a, b):
    lane = lax.broadcasted_iota(jnp.int32, a.shape, 1)
    return jnp.where(lane < S, a, pltpu.roll(b, S, 1))


def merge(stats):
    lane = lax.broadcasted_iota(jnp.int32, (8, 128), 1)
    top = stats[0]
    for s in stats[1:]:
        top = jnp.maximum(top, s)
    total = jnp.zeros((8, 128), F32)
    weights = []
    for s in stats:
        w = jnp.exp(jnp.where(lane < S, s - top, 0.0))
        weights.append(w)
        total = total + pltpu.roll(s, S, 1) * w
    return jnp.where(lane < S, top, 0.0), total, weights


def kernel(
    tokens_hbm, router_hbm, w_in_hbm, w_out_hbm, grad_hbm,
    mixed_v, d_tok_v, d_rout_v, d_w_in_v, d_w_out_v,
    tok, rout, w_in, w_out, grad,
    rc0, rc1, rc2, rc3, rm0, rm1, rm2, rm3, ry0, ry1, ry2, ry3, rr0, rr1, rr2, rr3,
    es0, es1, es2, es3, er0, er1, er2, er3, ag0, ag1, ag2, ag3,
    st_send, st_mid, st_core, st_recv, weight,
    tc_send, tc_mid, tc_sum, ty_send, ty_recv, tz_send, tz_recv,
    in_sem, send_sem, recv_sem, hello,
):
    rc, rm, ry, rr = (rc0, rc1, rc2, rc3), (rm0, rm1, rm2, rm3), (ry0, ry1, ry2, ry3), (rr0, rr1, rr2, rr3)
    es, er, ag = (es0, es1, es2, es3), (er0, er1, er2, er3), (ag0, ag1, ag2, ag3)
    me_s = lax.axis_index("seq")
    me_n = lax.axis_index("exp")
    y = me_s // 2
    core = lax.rem(me_s, 2)
    z = me_n // XS
    x = lax.rem(me_n, XS)
    twin = me_s + 1 - 2 * core
    partner = lax.rem(me_s - z + SEQ, SEQ)
    own = lax.rem(core + z, 2)
    away = 1 - own
    mine = partner // 2

    loads = [
        pltpu.make_async_copy(src, dst, in_sem.at[i])
        for i, (src, dst) in enumerate(
            ((router_hbm, rout), (grad_hbm, grad), (w_in_hbm, w_in), (w_out_hbm, w_out))
        )
    ]
    pieces = [
        pltpu.make_async_copy(
            tokens_hbm.at[pl.ds(128 * k, 128)], tok.at[pl.ds(128 * k, 128)], in_sem.at[4 + k]
        )
        for k in range(4)
    ]
    loads[0].start()
    for piece in pieces:
        piece.start()

    barrier = pltpu.get_barrier_semaphore()

    def greet(s, n):
        pl.semaphore_signal(barrier, inc=1, device_id=(s, n), device_id_type=MESH)

    def ex_peer(k):
        return XS * partner + k

    def yx_peer(k):
        return 2 * lax.rem(y + k // XS, YS) + core, XS * z + lax.rem(x + lax.rem(k, XS), XS)

    along_x = [XS * z + lax.rem(x + k, XS) for k in range(1, XS)]
    along_z = [XS * lax.rem(z + k, ZS) + x for k in NEAR]
    for k in range(1, YS):
        greet(2 * lax.rem(y + k, YS) + core, me_n)
    for n in along_x + along_z:
        greet(me_s, n)
    greet(twin, me_n)

    def pass_on(sem, devices):
        for n in devices:
            pl.semaphore_signal(
                hello.at[sem], inc=1, device_id=(me_s, n), device_id_type=MESH
            )

    def send(src, dst, sem, s, n):
        pltpu.make_async_remote_copy(
            src_ref=src, dst_ref=dst, send_sem=send_sem.at[sem], recv_sem=recv_sem.at[sem],
            device_id=(s, n), device_id_type=MESH,
        ).start()

    def all_of(ref, sem):
        pltpu.make_async_copy(ref, ref, sem).wait()

    def arrived(ref, sem):
        all_of(ref, recv_sem.at[sem])

    def over_y(make):
        for k in (2, 1, 3):
            make(2 * lax.rem(y + k, YS) + core)

    def rs_core(i):
        send(rc[i].at[away], rm[i], 5 * i, twin, me_n)

    def rs_y_send(i):
        rr[i][y] = ry[i][mine]
        over_y(
            lambda s: send(
                ry[i].at[lax.rem(s - z + SEQ, SEQ) // 2], rr[i].at[y], 5 * i + 1, s, me_n
            )
        )

    def rs_y(i):
        arrived(rm[i], 5 * i)
        for k in range(YS):
            ry[i][k] = (rc[i][own, k].astype(F32) + rm[i][k].astype(F32)).astype(ry[i].dtype)
        rs_y_send(i)

    def rs_total(i):
        arrived(rr[i].at[pl.ds(0, YS - 1)], 5 * i + 1)
        total = rr[i][0].astype(F32)
        for k in range(1, YS):
            total = total + rr[i][k].astype(F32)
        return total

    def ex_start(i, total, extra=None):
        rows = [total[:8], total[8:]]
        if extra is not None:
            rows.append(extra)
        rows = jnp.concatenate(rows, axis=1)
        for k in range(XS):
            es[i][k] = rows[2 * k : 2 * k + 2].astype(es[i].dtype)
        for k in (2, 1, 3):
            to = lax.rem(x + k, XS)
            send(es[i].at[to], er[i].at[x], 5 * i + 2, me_s, ex_peer(to))

        @pl.when(partner != z)
        def _():
            send(es[i].at[x], er[i].at[x], 5 * i + 2, me_s, ex_peer(x))

        @pl.when(partner == z)
        def _():
            er[i][x] = es[i][x]

    def ex_rows(i):
        @pl.when(partner != z)
        def _():
            arrived(er[i], 5 * i + 2)

        @pl.when(partner == z)
        def _():
            arrived(er[i].at[pl.ds(0, XS - 1)], 5 * i + 2)

        return jnp.concatenate([er[i][k].astype(F32) for k in range(XS)], axis=0)

    def ag_start(i, rows):
        piece = jnp.concatenate([rows[:, :H], rows[:, H:D]], axis=0)
        if rows.shape[1] > D:
            extra = jnp.concatenate([rows[:, D:], jnp.zeros((8, 128), F32)], axis=0)
            piece = jnp.concatenate([piece, extra], axis=1)
        ag[i][4 * own + mine] = piece.astype(BF16)
        if i in DIRECT:
            for k in (4, 5, 3, 2, 6, 7, 1):
                send(
                    ag[i].at[4 * own + mine], ag[i].at[4 * own + mine], 5 * i + 3, lax.rem(me_s + k, SEQ), me_n
                )
        else:
            over_y(lambda s: send(ag[i].at[4 * own + mine], ag[i].at[4 * own + mine], 5 * i + 3, s, me_n))

    def ag_core(i):
        if i in DIRECT:
            return
        arrived(ag[i].at[pl.ds(0, YS - 1)], 5 * i + 3)
        half = ag[i].at[pl.ds(pl.multiple_of(4 * own, 4), 4)]
        send(half, half, 5 * i + 4, twin, me_n)

    def ag_finish(i):
        if i in DIRECT:
            arrived(ag[i].at[pl.ds(0, SEQ - 1)], 5 * i + 3)
        else:
            arrived(ag[i].at[pl.ds(0, YS)], 5 * i + 4)
        return load_blocks(ag[i])

    loads[0].wait()
    for piece in pieces:
        piece.wait()
    for load in loads[1:]:
        load.start()
    router_t = rout[...]
    logits = nt(router_t, tok[...])
    own_top = jnp.max(logits, axis=1, keepdims=True)
    own_exp = jnp.exp(logits - own_top)
    st_send[...] = pair_rows(own_top, jnp.sum(own_exp, axis=1, keepdims=True))
    exp_high, exp_low = split(own_exp)
    store_blocks(rc[1], nn(exp_high, tok[...]) + nn(exp_low, tok[...]))

    pl.semaphore_wait(barrier, 1 + YS - 1 + XS - 1 + len(NEAR))
    rs_core(1)
    send(st_send, st_mid, 20, twin, me_n)
    pass_on(0, along_x + along_z)
    row_exp = jnp.exp(logits - jnp.max(logits, axis=0, keepdims=True))
    combine = row_exp / jnp.sum(row_exp, axis=0, keepdims=True)
    loads[1].wait()
    store_blocks(rc[0], nn(combine.astype(BF16), grad[...]))
    rs_core(0)

    arrived(st_mid, 20)
    top, total, (w_own, w_mid) = merge([st_send[...], st_mid[...]])
    st_core[...] = left(top, total)
    weight[...] = columns(left(w_own, w_mid))
    arrived(rm[1], 5)
    for k in range(YS):
        g = pl.multiple_of(8 * (own + 2 * k), 8)
        a = weight[pl.ds(g, 8)]
        b = weight[pl.ds(S + g, 8)]
        a = jnp.concatenate([jnp.concatenate([a] * 5, axis=1)] * 2, axis=0)
        b = jnp.concatenate([jnp.concatenate([b] * 5, axis=1)] * 2, axis=0)
        ry[1][k] = rc[1][own, k] * a + rm[1][k] * b
    st_recv[y] = st_core[...]
    over_y(lambda s: send(st_core, st_recv.at[y], 21, s, me_n))
    rs_y_send(1)
    rs_y(0)
    pl.semaphore_wait(hello.at[0], XS - 1 + len(NEAR))
    pass_on(1, along_z)

    arrived(st_recv.at[pl.ds(0, YS - 1)], 21)
    stats = [st_recv[k] for k in range(YS)]
    top, total, ws = merge(stats)
    w = [v / total for v in ws]
    weight[...] = columns(left(w[0], w[1]))
    g = pl.multiple_of(8 * partner, 8)
    w0, w1 = weight[pl.ds(g, 8)], weight[pl.ds(S + g, 8)]
    weight[...] = columns(left(w[2], w[3]))
    w2, w3 = weight[pl.ds(g, 8)], weight[pl.ds(S + g, 8)]
    arrived(rr[1].at[pl.ds(0, YS - 1)], 6)
    total_in = jnp.zeros((16, H), F32)
    for k, v in enumerate((w0, w1, w2, w3)):
        total_in = total_in + rr[1][k] * jnp.concatenate([jnp.concatenate([v] * 5, axis=1)] * 2, axis=0)
    pl.semaphore_wait(hello.at[1], len(NEAR))
    ex_start(1, total_in)
    ex_start(0, rs_total(0))
    scale = columns(left(jnp.exp(st_send[...] - top) / total, total))[:S, :1]
    dispatch = own_exp * scale

    rows_1 = ex_rows(1)
    ag_start(1, rows_1)
    ag_start(0, ex_rows(0))
    ag_core(1)
    ag_core(0)

    loads[2].wait()
    rows = ag_finish(1)
    hidden = nn(rows, w_in[...])
    cdf = 0.5 * (1.0 + lax.erf(hidden * (1.0 / math.sqrt(2.0))))
    act = hidden * cdf
    loads[3].wait()
    store_blocks(rc[3], nn(act.astype(BF16), w_out[...]))
    rs_core(3)
    pdf = jnp.exp(-0.5 * hidden * hidden) * (1.0 / math.sqrt(2.0 * math.pi))
    slope = cdf + hidden * pdf
    d_rows = ag_finish(0)
    d_hidden_b = (nt(d_rows, w_out[...]) * slope).astype(BF16)
    store_blocks(rc[2], nt(d_hidden_b, w_in[...]))
    rs_core(2)

    rs_y(3)
    rs_y(2)
    act_t = act.T.astype(BF16)
    for k in range(5):
        part = slice(128 * k, 128 * k + 128)
        d_w_out_v[part] = nn(act_t[part], d_rows).astype(BF16)
    ex_start(3, rs_total(3))
    total = rs_total(2).astype(BF16).astype(F32)
    column = jnp.sum(total[:8] * rows_1[:, :H] + total[8:] * rows_1[:, H:], axis=1, keepdims=True)
    ex_start(2, total, thirds(column))
    rows_t = rows.astype(F32).T.astype(BF16)
    for k in range(10):
        part = slice(128 * k, 128 * k + 128)
        d_w_in_v[part] = nn(rows_t[part], d_hidden_b).astype(BF16)
    ag_start(3, ex_rows(3))
    ag_start(2, ex_rows(2))
    ag_core(3)
    ag_core(2)

    slots_out = ag_finish(3)
    d_combine = nt(slots_out, grad[...])
    d_logit_c = combine * (d_combine - jnp.sum(combine * d_combine, axis=0, keepdims=True))
    d_slots = ag_finish(2)
    column = jnp.concatenate(
        [ag[2][4 * (g % 2) + g // 2, :8, H:].astype(F32) for g in range(SEQ)], axis=0
    )
    column = jnp.sum(column, axis=1, keepdims=True)
    d_dispatch = nt(d_slots, tok[...])
    d_logit = d_logit_c + dispatch * (d_dispatch - column)

    d_router_t = nn(d_logit.astype(BF16), tok[...])
    pair = jnp.concatenate([d_router_t, pltpu.roll(d_router_t, D - 80, 1)], axis=0).T
    for k in range(SEQ):
        tc_send[k % 2, k // 2] = pair[160 * k : 160 * k + 80]
    send(tc_send.at[1 - core], tc_mid, 22, twin, me_n)
    combine_t = combine.T.astype(BF16)
    for k in range(4):
        part = slice(128 * k, 128 * k + 128)
        mixed_v[part] = nn(combine_t[part], slots_out).astype(BF16)
    arrived(tc_mid, 22)
    for k in range(YS):
        tc_sum[k] = tc_send[core, k] + tc_mid[k]
    for k in range(YS):
        for j in range(XS):
            for i in range(5):
                ty_send[k, j, i] = tc_sum[k, pl.ds(5 * j + i, 4, stride=20), :]
    ty_recv[XS * y + x] = ty_send[y, x]

    for k in (10, 9, 11, 6, 14, 8, 2, 5, 7, 13, 15, 4, 12, 1, 3):
        s, n = yx_peer(k)
        send(ty_send.at[s // 2, lax.rem(n, XS)], ty_recv.at[XS * y + x], 23, s, n)
    weights = jnp.concatenate([dispatch, d_logit], axis=0).T.astype(BF16)
    values = jnp.concatenate([d_slots, router_t], axis=0)
    for k in range(4):
        part = slice(128 * k, 128 * k + 128)
        d_tok_v[part] = nn(weights[part], values).astype(BF16)
    arrived(ty_recv.at[pl.ds(0, YS * XS - 1)], 23)
    total = ty_recv[0]
    for k in range(1, YS * XS):
        total = total + ty_recv[k]
    tz_send[...] = jnp.zeros((ZS, 4, 128), F32)
    for k in range(3):
        first = total[2 * k]
        second = total[2 * k + 1] if k < 2 else jnp.zeros((4, 128), F32)
        for half, packed in enumerate((left(first, second), left(pltpu.roll(first, S, 1), pltpu.roll(second, S, 1)))):
            for i in range(4):
                tz_send[4 * half + i, k : k + 1] = packed[i : i + 1]
    tz_recv[z] = tz_send[z]

    for k in (4, 3, 5, 2, 6, 1, 7):
        to = lax.rem(z + k, ZS)
        send(tz_send.at[to], tz_recv.at[z], 24, me_s, XS * to + x)

    arrived(tz_recv.at[pl.ds(0, ZS - 1)], 24)
    total = tz_recv[0]
    for k in range(1, ZS):
        total = total + tz_recv[k]
    other = pltpu.roll(total, S, 1)
    for k in range(5):
        d_rout_v[k : k + 1] = (other if k % 2 else total)[k // 2 : k // 2 + 1, :S]

    for i in range(4):
        all_of(rm[i], send_sem.at[5 * i])
        all_of(rr[i].at[pl.ds(0, YS - 1)], send_sem.at[5 * i + 1])

        @pl.when(partner != z)
        def _():
            all_of(er[i], send_sem.at[5 * i + 2])

        @pl.when(partner == z)
        def _():
            all_of(er[i].at[pl.ds(0, XS - 1)], send_sem.at[5 * i + 2])

        if i in DIRECT:
            all_of(ag[i].at[pl.ds(0, SEQ - 1)], send_sem.at[5 * i + 3])
        else:
            all_of(ag[i].at[pl.ds(0, YS - 1)], send_sem.at[5 * i + 3])
            all_of(ag[i].at[pl.ds(0, YS)], send_sem.at[5 * i + 4])
    all_of(st_mid, send_sem.at[20])
    all_of(st_recv.at[pl.ds(0, YS - 1)], send_sem.at[21])
    all_of(tc_mid, send_sem.at[22])
    all_of(ty_recv.at[pl.ds(0, YS * XS - 1)], send_sem.at[23])
    all_of(tz_recv.at[pl.ds(0, ZS - 1)], send_sem.at[24])


def store(a0, a1, a2, a3, a4, b0, b1, b2, b3, b4, sem):
    copies = [
        pltpu.make_async_copy(a, b, sem.at[i])
        for i, (a, b) in enumerate(((a0, b0), (a1, b1), (a2, b2), (a3, b3), (a4, b4)))
    ]
    for copy in copies:
        copy.start()
    for copy in copies:
        copy.wait()


def shards(tokens, router, w_in, w_out, grad_out):
    any_space = pl.BlockSpec(memory_space=pl.ANY)
    dma = pltpu.SemaphoreType.DMA
    vmem = pltpu.VMEM
    kinds = (BF16, F32, BF16, BF16)
    wide = (0, 0, 128, 0)
    results = pl.pallas_call(
        kernel,
        out_shape=(
            vmem((T, D), BF16),
            vmem((T, D), BF16),
            vmem((5, S), F32),
            vmem((D, H), BF16),
            vmem((H, D), BF16),
        ),
        in_specs=[any_space] * 5,
        out_specs=[pl.BlockSpec(memory_space=vmem)] * 5,
        scratch_shapes=[
            vmem((T, D), BF16),
            vmem((S, D), BF16),
            vmem((D, H), BF16),
            vmem((H, D), BF16),
            vmem((T, D), BF16),
            *[vmem((2, 4, 16, H), k) for k in kinds],
            *[vmem((4, 16, H), k) for k in kinds],
            *[vmem((4, 16, H), k) for k in kinds],
            *[vmem((4, 16, H), k) for k in kinds],
            *[vmem((XS, 2, D + w), k) for w, k in zip(wide, kinds)],
            *[vmem((XS, 2, D + w), k) for w, k in zip(wide, kinds)],
            *[vmem((SEQ, 16, H + w), BF16) for w in wide],
            vmem((8, 128), F32),
            vmem((8, 128), F32),
            vmem((8, 128), F32),
            vmem((YS, 8, 128), F32),
            vmem((128, 128), F32),
            vmem((2, YS, 80, 128), F32),
            vmem((YS, 80, 128), F32),
            vmem((YS, 80, 128), F32),
            vmem((YS, XS, 5, 4, 128), F32),
            vmem((YS * XS, 5, 4, 128), F32),
            vmem((ZS, 4, 128), F32),
            vmem((ZS, 4, 128), F32),
            dma((8,)), dma((25,)), dma((25,)), pltpu.SemaphoreType.REGULAR((2,)),
        ],
        compiler_params=pltpu.CompilerParams(
            collective_id=0, has_side_effects=True, vmem_limit_bytes=VMEM
        ),
    )(tokens[0], router.T, w_in[0], w_out[0], grad_out[0])
    mixed, d_tokens, d_router, d_w_in, d_w_out = pl.pallas_call(
        store,
        out_shape=tuple(jax.ShapeDtypeStruct(r.shape, r.dtype) for r in results),
        in_specs=[pl.BlockSpec(memory_space=vmem)] * 5,
        out_specs=[any_space] * 5,
        scratch_shapes=[dma((5,))],
        compiler_params=pltpu.CompilerParams(vmem_limit_bytes=4 * 1024 * 1024),
    )(*results)
    return mixed[None], d_tokens[None], d_router, d_w_in[None], d_w_out[None]


def solution(mesh):
    in_specs = (
        P("exp", "seq", None),
        P(),
        P("exp", None, "seq"),
        P("exp", "seq", None),
        P("exp", "seq", None),
    )
    out_specs = (
        P("exp", "seq", None),
        P("exp", "seq", None),
        P(("seq", "exp"), None),
        P("exp", None, "seq"),
        P("exp", "seq", None),
    )
    return jax.shard_map(shards, mesh=mesh, in_specs=in_specs, out_specs=out_specs, check_vma=False)
```

```python
import math

import jax
import jax.numpy as jnp
from jax import lax
from jax.experimental import pallas as pl
from jax.experimental.pallas import tpu as pltpu
from jax.sharding import PartitionSpec as P

F32 = jnp.float32
BF16 = jnp.bfloat16
MESH = pl.DeviceIdType.MESH
SEQ = 8
YS = 4
XS = 4
ZS = 8
DIRECT = (0, 1, 2)
NEAR = (1, 2, ZS - 2, ZS - 1)
D = 1280
H = 640
T = 512
S = 64
VMEM = 52 * 1024 * 1024


def nn(a, b):
    return lax.dot_general(a, b, (((1,), (0,)), ((), ())), preferred_element_type=F32)


def nt(a, b):
    return lax.dot_general(a, b, (((1,), (1,)), ((), ())), preferred_element_type=F32)


def split(a):
    high = a.astype(BF16)
    return high, (a - high.astype(F32)).astype(BF16)


def thirds(column):
    value = jnp.broadcast_to(column, (8, 128))
    high, rest = split(value)
    middle, low = split(value - high.astype(F32))
    lane = lax.broadcasted_iota(jnp.int32, (8, 128), 1)
    value = jnp.where(lane == 2, low.astype(F32), 0.0)
    value = jnp.where(lane == 1, middle.astype(F32), value)
    return jnp.where(lane == 0, high.astype(F32), value)


def block(a, g):
    rows = a[8 * g : 8 * g + 8]
    return jnp.concatenate([rows[:, :H], rows[:, H:]], axis=0)


def store_blocks(ref, a):
    for g in range(SEQ):
        ref[g % 2, g // 2] = block(a, g).astype(ref.dtype)


def load_blocks(ref):
    parts = [ref[4 * (g % 2) + g // 2].astype(F32) for g in range(SEQ)]
    lo = jnp.concatenate([p[:8, :H] for p in parts], axis=0)
    hi = jnp.concatenate([p[8:, :H] for p in parts], axis=0)
    return jnp.concatenate([lo, hi], axis=1).astype(BF16)


def pair_rows(top, low):
    square = jnp.concatenate(
        [jnp.broadcast_to(top, (S, 128)), jnp.broadcast_to(low, (S, 128))], axis=0
    )
    return square.T[:8]


def columns(rows):
    return jnp.concatenate([rows] * 16, axis=0).T


def left(a, b):
    lane = lax.broadcasted_iota(jnp.int32, a.shape, 1)
    return jnp.where(lane < S, a, pltpu.roll(b, S, 1))


def merge(stats):
    lane = lax.broadcasted_iota(jnp.int32, (8, 128), 1)
    top = stats[0]
    for s in stats[1:]:
        top = jnp.maximum(top, s)
    total = jnp.zeros((8, 128), F32)
    weights = []
    for s in stats:
        w = jnp.exp(jnp.where(lane < S, s - top, 0.0))
        weights.append(w)
        total = total + pltpu.roll(s, S, 1) * w
    return jnp.where(lane < S, top, 0.0), total, weights


def kernel(
    tokens_hbm, router_hbm, w_in_hbm, w_out_hbm, grad_hbm,
    mixed_v, d_tok_v, d_rout_v, d_w_in_v, d_w_out_v,
    tok, rout, w_in, w_out, grad,
    rc0, rc1, rc2, rc3, rc4, rm0, rm1, rm2, rm3, rm4, ry0, ry1, ry2, ry3, ry4, rr0, rr1, rr2, rr3, rr4,
    es0, es1, es2, es3, es4, er0, er1, er2, er3, er4, ag0, ag1, ag2, ag3,
    st_send, st_mid, st_core, st_recv, weight,
    tc_send, tc_mid, tc_sum, ty_send, ty_recv, tz_send, tz_recv,
    in_sem, send_sem, recv_sem, hello,
):
    rc, rm = (rc0, rc1, rc2, rc3, rc4), (rm0, rm1, rm2, rm3, rm4)
    ry, rr = (ry0, ry1, ry2, ry3, ry4), (rr0, rr1, rr2, rr3, rr4)
    es, er, ag = (es0, es1, es2, es3, es4), (er0, er1, er2, er3, er4), (ag0, ag1, ag2, ag3)
    me_s = lax.axis_index("seq")
    me_n = lax.axis_index("exp")
    y = me_s // 2
    core = lax.rem(me_s, 2)
    z = me_n // XS
    x = lax.rem(me_n, XS)
    twin = me_s + 1 - 2 * core
    partner = lax.rem(me_s - z + SEQ, SEQ)
    own = lax.rem(core + z, 2)
    away = 1 - own
    mine = partner // 2

    loads = [
        pltpu.make_async_copy(src, dst, in_sem.at[i])
        for i, (src, dst) in enumerate(
            ((router_hbm, rout), (grad_hbm, grad), (w_in_hbm, w_in), (w_out_hbm, w_out))
        )
    ]
    pieces = [
        pltpu.make_async_copy(
            tokens_hbm.at[pl.ds(128 * k, 128)], tok.at[pl.ds(128 * k, 128)], in_sem.at[4 + k]
        )
        for k in range(4)
    ]
    loads[0].start()
    for piece in pieces:
        piece.start()

    barrier = pltpu.get_barrier_semaphore()

    def greet(s, n):
        pl.semaphore_signal(barrier, inc=1, device_id=(s, n), device_id_type=MESH)

    def ex_peer(k):
        return XS * partner + k

    def yx_peer(k):
        return 2 * lax.rem(y + k // XS, YS) + core, XS * z + lax.rem(x + lax.rem(k, XS), XS)

    along_x = [XS * z + lax.rem(x + k, XS) for k in range(1, XS)]
    along_z = [XS * lax.rem(z + k, ZS) + x for k in NEAR]
    for k in range(1, YS):
        greet(2 * lax.rem(y + k, YS) + core, me_n)
    for n in along_x + along_z:
        greet(me_s, n)
    greet(twin, me_n)

    def pass_on(sem, devices):
        for n in devices:
            pl.semaphore_signal(
                hello.at[sem], inc=1, device_id=(me_s, n), device_id_type=MESH
            )

    def send(src, dst, sem, s, n):
        pltpu.make_async_remote_copy(
            src_ref=src, dst_ref=dst, send_sem=send_sem.at[sem], recv_sem=recv_sem.at[sem],
            device_id=(s, n), device_id_type=MESH,
        ).start()

    def all_of(ref, sem):
        pltpu.make_async_copy(ref, ref, sem).wait()

    def arrived(ref, sem):
        all_of(ref, recv_sem.at[sem])

    def over_y(make):
        for k in (2, 1, 3):
            make(2 * lax.rem(y + k, YS) + core)

    def rs_core(i):
        send(rc[i].at[away], rm[i], 5 * i, twin, me_n)

    def rs_y_send(i):
        rr[i][y] = ry[i][mine]
        over_y(
            lambda s: send(
                ry[i].at[lax.rem(s - z + SEQ, SEQ) // 2], rr[i].at[y], 5 * i + 1, s, me_n
            )
        )

    def rs_y(i):
        arrived(rm[i], 5 * i)
        for k in range(YS):
            ry[i][k] = (rc[i][own, k].astype(F32) + rm[i][k].astype(F32)).astype(ry[i].dtype)
        rs_y_send(i)

    def rs_total(i):
        arrived(rr[i].at[pl.ds(0, YS - 1)], 5 * i + 1)
        total = rr[i][0].astype(F32)
        for k in range(1, YS):
            total = total + rr[i][k].astype(F32)
        return total

    def ex_start(i, total, extra=None):
        rows = [total[:8], total[8:]]
        if extra is not None:
            rows.append(extra)
        rows = jnp.concatenate(rows, axis=1)
        for k in range(XS):
            es[i][k] = rows[2 * k : 2 * k + 2].astype(es[i].dtype)
        for k in (2, 1, 3):
            to = lax.rem(x + k, XS)
            send(es[i].at[to], er[i].at[x], 5 * i + 2, me_s, ex_peer(to))

        @pl.when(partner != z)
        def _():
            send(es[i].at[x], er[i].at[x], 5 * i + 2, me_s, ex_peer(x))

        @pl.when(partner == z)
        def _():
            er[i][x] = es[i][x]

    def ex_rows(i):
        @pl.when(partner != z)
        def _():
            arrived(er[i], 5 * i + 2)

        @pl.when(partner == z)
        def _():
            arrived(er[i].at[pl.ds(0, XS - 1)], 5 * i + 2)

        return jnp.concatenate([er[i][k].astype(F32) for k in range(XS)], axis=0)

    def ag_start(i, rows):
        piece = jnp.concatenate([rows[:, :H], rows[:, H:D]], axis=0)
        if rows.shape[1] > D:
            extra = jnp.concatenate([rows[:, D:], jnp.zeros((8, 128), F32)], axis=0)
            piece = jnp.concatenate([piece, extra], axis=1)
        ag[i][4 * own + mine] = piece.astype(BF16)
        if i in DIRECT:
            for k in (4, 5, 3, 2, 6, 7, 1):
                send(
                    ag[i].at[4 * own + mine], ag[i].at[4 * own + mine], 5 * i + 3, lax.rem(me_s + k, SEQ), me_n
                )
        else:
            over_y(lambda s: send(ag[i].at[4 * own + mine], ag[i].at[4 * own + mine], 5 * i + 3, s, me_n))

    def ag_core(i):
        if i in DIRECT:
            return
        arrived(ag[i].at[pl.ds(0, YS - 1)], 5 * i + 3)
        half = ag[i].at[pl.ds(pl.multiple_of(4 * own, 4), 4)]
        send(half, half, 5 * i + 4, twin, me_n)

    def ag_finish(i):
        if i in DIRECT:
            arrived(ag[i].at[pl.ds(0, SEQ - 1)], 5 * i + 3)
        else:
            arrived(ag[i].at[pl.ds(0, YS)], 5 * i + 4)
        return load_blocks(ag[i])

    loads[0].wait()
    for piece in pieces:
        piece.wait()
    for load in loads[1:]:
        load.start()
    router_t = rout[...]
    logits = nt(router_t, tok[...])
    own_top = jnp.max(logits, axis=1, keepdims=True)
    own_exp = jnp.exp(logits - own_top)
    st_send[...] = pair_rows(own_top, jnp.sum(own_exp, axis=1, keepdims=True))
    exp_high, exp_low = split(own_exp)
    in_part = nn(exp_high, tok[...]) + nn(exp_low, tok[...])
    store_blocks(rc[1], in_part)

    pl.semaphore_wait(barrier, 1 + YS - 1 + XS - 1 + len(NEAR))
    rs_core(1)
    send(st_send, st_mid, 25, twin, me_n)
    pass_on(0, along_x + along_z)
    row_exp = jnp.exp(logits - jnp.max(logits, axis=0, keepdims=True))
    combine = row_exp / jnp.sum(row_exp, axis=0, keepdims=True)
    loads[1].wait()
    store_blocks(rc[0], nn(combine.astype(BF16), grad[...]))
    rs_core(0)
    store_blocks(rc[4], split(in_part)[1])
    rs_core(4)

    arrived(st_mid, 25)
    top, total, (w_own, w_mid) = merge([st_send[...], st_mid[...]])
    st_core[...] = left(top, total)
    weight[...] = columns(left(w_own, w_mid))

    def spread(w):
        return jnp.concatenate([jnp.concatenate([w] * 5, axis=1)] * 2, axis=0)

    def weighted(i, k):
        g = pl.multiple_of(8 * (own + 2 * k), 8)
        a, b = spread(weight[pl.ds(g, 8)]), spread(weight[pl.ds(S + g, 8)])
        return rc[i][own, k].astype(F32) * a + rm[i][k].astype(F32) * b

    arrived(rm[1], 5)
    for k in range(YS):
        ry[1][k] = weighted(1, k).astype(BF16)
    st_recv[y] = st_core[...]
    over_y(lambda s: send(st_core, st_recv.at[y], 26, s, me_n))
    rs_y_send(1)
    rs_y(0)
    pl.semaphore_wait(hello.at[0], XS - 1 + len(NEAR))
    pass_on(1, along_z)
    arrived(rm[4], 20)
    for k in range(YS):
        ry[4][k] = (split(weighted(1, k))[1].astype(F32) + weighted(4, k)).astype(BF16)
    rs_y_send(4)

    arrived(st_recv.at[pl.ds(0, YS - 1)], 26)
    stats = [st_recv[k] for k in range(YS)]
    top, total, ws = merge(stats)
    w = [v / total for v in ws]
    weight[...] = columns(left(w[0], w[1]))
    g = pl.multiple_of(8 * partner, 8)
    w0, w1 = weight[pl.ds(g, 8)], weight[pl.ds(S + g, 8)]
    weight[...] = columns(left(w[2], w[3]))
    w2, w3 = weight[pl.ds(g, 8)], weight[pl.ds(S + g, 8)]
    arrived(rr[1].at[pl.ds(0, YS - 1)], 6)
    total_in = jnp.zeros((16, H), F32)
    for k, v in enumerate((w0, w1, w2, w3)):
        total_in = total_in + rr[1][k].astype(F32) * spread(v)
    pl.semaphore_wait(hello.at[1], len(NEAR))
    ex_start(1, total_in)
    ex_start(0, rs_total(0))
    scale = columns(left(jnp.exp(st_send[...] - top) / total, total))[:S, :1]
    dispatch = own_exp * scale
    arrived(rr[4].at[pl.ds(0, YS - 1)], 21)
    total_low = split(total_in)[1].astype(F32)
    for k, v in enumerate((w0, w1, w2, w3)):
        total_low = total_low + rr[4][k].astype(F32) * spread(v)
    ex_start(4, total_low)

    rows_1 = ex_rows(1)
    ag_start(1, rows_1)
    ag_start(0, ex_rows(0))
    ag_core(1)
    ag_core(0)

    loads[2].wait()
    rows = ag_finish(1)
    hidden = nn(rows, w_in[...])
    cdf = 0.5 * (1.0 + lax.erf(hidden * (1.0 / math.sqrt(2.0))))
    act = hidden * cdf
    loads[3].wait()
    store_blocks(rc[3], nn(act.astype(BF16), w_out[...]))
    rs_core(3)
    pdf = jnp.exp(-0.5 * hidden * hidden) * (1.0 / math.sqrt(2.0 * math.pi))
    slope = cdf + hidden * pdf
    d_rows = ag_finish(0)
    d_hidden_b = (nt(d_rows, w_out[...]) * slope).astype(BF16)
    store_blocks(rc[2], nt(d_hidden_b, w_in[...]))
    rs_core(2)

    rs_y(3)
    rs_y(2)
    act_t = act.T.astype(BF16)
    for k in range(5):
        part = slice(128 * k, 128 * k + 128)
        d_w_out_v[part] = nn(act_t[part], d_rows).astype(BF16)
    ex_start(3, rs_total(3))
    total = rs_total(2).astype(BF16).astype(F32)
    rows_1 = rows_1 + ex_rows(4)
    column = jnp.sum(total[:8] * rows_1[:, :H] + total[8:] * rows_1[:, H:], axis=1, keepdims=True)
    ex_start(2, total, thirds(column))
    rows_t = rows.astype(F32).T.astype(BF16)
    for k in range(10):
        part = slice(128 * k, 128 * k + 128)
        d_w_in_v[part] = nn(rows_t[part], d_hidden_b).astype(BF16)
    ag_start(3, ex_rows(3))
    ag_start(2, ex_rows(2))
    ag_core(3)
    ag_core(2)

    slots_out = ag_finish(3)
    d_combine = nt(slots_out, grad[...])
    d_logit_c = combine * (d_combine - jnp.sum(combine * d_combine, axis=0, keepdims=True))
    d_slots = ag_finish(2)
    column = jnp.concatenate(
        [ag[2][4 * (g % 2) + g // 2, :8, H:].astype(F32) for g in range(SEQ)], axis=0
    )
    column = jnp.sum(column, axis=1, keepdims=True)
    d_dispatch = nt(d_slots, tok[...])
    d_logit = d_logit_c + dispatch * (d_dispatch - column)

    d_router_t = nn(d_logit.astype(BF16), tok[...])
    pair = jnp.concatenate([d_router_t, pltpu.roll(d_router_t, D - 80, 1)], axis=0).T
    for k in range(SEQ):
        tc_send[k % 2, k // 2] = pair[160 * k : 160 * k + 80]
    send(tc_send.at[1 - core], tc_mid, 27, twin, me_n)
    combine_t = combine.T.astype(BF16)
    for k in range(4):
        part = slice(128 * k, 128 * k + 128)
        mixed_v[part] = nn(combine_t[part], slots_out).astype(BF16)
    arrived(tc_mid, 27)
    for k in range(YS):
        tc_sum[k] = tc_send[core, k] + tc_mid[k]
    for k in range(YS):
        for j in range(XS):
            for i in range(5):
                ty_send[k, j, i] = tc_sum[k, pl.ds(5 * j + i, 4, stride=20), :]
    ty_recv[XS * y + x] = ty_send[y, x]

    for k in (10, 9, 11, 6, 14, 8, 2, 5, 7, 13, 15, 4, 12, 1, 3):
        s, n = yx_peer(k)
        send(ty_send.at[s // 2, lax.rem(n, XS)], ty_recv.at[XS * y + x], 28, s, n)
    weights = jnp.concatenate([dispatch, d_logit], axis=0).T.astype(BF16)
    values = jnp.concatenate([d_slots, router_t], axis=0)
    for k in range(4):
        part = slice(128 * k, 128 * k + 128)
        d_tok_v[part] = nn(weights[part], values).astype(BF16)
    arrived(ty_recv.at[pl.ds(0, YS * XS - 1)], 28)
    total = ty_recv[0]
    for k in range(1, YS * XS):
        total = total + ty_recv[k]
    tz_send[...] = jnp.zeros((ZS, 4, 128), F32)
    for k in range(3):
        first = total[2 * k]
        second = total[2 * k + 1] if k < 2 else jnp.zeros((4, 128), F32)
        for half, packed in enumerate((left(first, second), left(pltpu.roll(first, S, 1), pltpu.roll(second, S, 1)))):
            for i in range(4):
                tz_send[4 * half + i, k : k + 1] = packed[i : i + 1]
    tz_recv[z] = tz_send[z]

    for k in (4, 3, 5, 2, 6, 1, 7):
        to = lax.rem(z + k, ZS)
        send(tz_send.at[to], tz_recv.at[z], 29, me_s, XS * to + x)

    arrived(tz_recv.at[pl.ds(0, ZS - 1)], 29)
    total = tz_recv[0]
    for k in range(1, ZS):
        total = total + tz_recv[k]
    other = pltpu.roll(total, S, 1)
    for k in range(5):
        d_rout_v[k : k + 1] = (other if k % 2 else total)[k // 2 : k // 2 + 1, :S]

    for i in range(5):
        all_of(rm[i], send_sem.at[5 * i])
        all_of(rr[i].at[pl.ds(0, YS - 1)], send_sem.at[5 * i + 1])

        @pl.when(partner != z)
        def _():
            all_of(er[i], send_sem.at[5 * i + 2])

        @pl.when(partner == z)
        def _():
            all_of(er[i].at[pl.ds(0, XS - 1)], send_sem.at[5 * i + 2])

        if i == 4:
            continue
        if i in DIRECT:
            all_of(ag[i].at[pl.ds(0, SEQ - 1)], send_sem.at[5 * i + 3])
        else:
            all_of(ag[i].at[pl.ds(0, YS - 1)], send_sem.at[5 * i + 3])
            all_of(ag[i].at[pl.ds(0, YS)], send_sem.at[5 * i + 4])
    all_of(st_mid, send_sem.at[25])
    all_of(st_recv.at[pl.ds(0, YS - 1)], send_sem.at[26])
    all_of(tc_mid, send_sem.at[27])
    all_of(ty_recv.at[pl.ds(0, YS * XS - 1)], send_sem.at[28])
    all_of(tz_recv.at[pl.ds(0, ZS - 1)], send_sem.at[29])


def store(a0, a1, a2, a3, a4, b0, b1, b2, b3, b4, sem):
    copies = [
        pltpu.make_async_copy(a, b, sem.at[i])
        for i, (a, b) in enumerate(((a0, b0), (a1, b1), (a2, b2), (a3, b3), (a4, b4)))
    ]
    for copy in copies:
        copy.start()
    for copy in copies:
        copy.wait()


def shards(tokens, router, w_in, w_out, grad_out):
    any_space = pl.BlockSpec(memory_space=pl.ANY)
    dma = pltpu.SemaphoreType.DMA
    vmem = pltpu.VMEM
    wide = (0, 0, 128, 0)
    rest = (0,)
    results = pl.pallas_call(
        kernel,
        out_shape=(
            vmem((T, D), BF16),
            vmem((T, D), BF16),
            vmem((5, S), F32),
            vmem((D, H), BF16),
            vmem((H, D), BF16),
        ),
        in_specs=[any_space] * 5,
        out_specs=[pl.BlockSpec(memory_space=vmem)] * 5,
        scratch_shapes=[
            vmem((T, D), BF16),
            vmem((S, D), BF16),
            vmem((D, H), BF16),
            vmem((H, D), BF16),
            vmem((T, D), BF16),
            *[vmem((2, 4, 16, H), BF16) for _ in wide + rest],
            *[vmem((4, 16, H), BF16) for _ in wide + rest],
            *[vmem((4, 16, H), BF16) for _ in wide + rest],
            *[vmem((4, 16, H), BF16) for _ in wide + rest],
            *[vmem((XS, 2, D + w), BF16) for w in wide + rest],
            *[vmem((XS, 2, D + w), BF16) for w in wide + rest],
            *[vmem((SEQ, 16, H + w), BF16) for w in wide],
            vmem((8, 128), F32),
            vmem((8, 128), F32),
            vmem((8, 128), F32),
            vmem((YS, 8, 128), F32),
            vmem((128, 128), F32),
            vmem((2, YS, 80, 128), F32),
            vmem((YS, 80, 128), F32),
            vmem((YS, 80, 128), F32),
            vmem((YS, XS, 5, 4, 128), F32),
            vmem((YS * XS, 5, 4, 128), F32),
            vmem((ZS, 4, 128), F32),
            vmem((ZS, 4, 128), F32),
            dma((8,)), dma((30,)), dma((30,)), pltpu.SemaphoreType.REGULAR((2,)),
        ],
        compiler_params=pltpu.CompilerParams(
            collective_id=0, has_side_effects=True, vmem_limit_bytes=VMEM
        ),
    )(tokens[0], router.T, w_in[0], w_out[0], grad_out[0])
    mixed, d_tokens, d_router, d_w_in, d_w_out = pl.pallas_call(
        store,
        out_shape=tuple(jax.ShapeDtypeStruct(r.shape, r.dtype) for r in results),
        in_specs=[pl.BlockSpec(memory_space=vmem)] * 5,
        out_specs=[any_space] * 5,
        scratch_shapes=[dma((5,))],
        compiler_params=pltpu.CompilerParams(vmem_limit_bytes=4 * 1024 * 1024),
    )(*results)
    return mixed[None], d_tokens[None], d_router, d_w_in[None], d_w_out[None]


def solution(mesh):
    in_specs = (
        P("exp", "seq", None),
        P(),
        P("exp", None, "seq"),
        P("exp", "seq", None),
        P("exp", "seq", None),
    )
    out_specs = (
        P("exp", "seq", None),
        P("exp", "seq", None),
        P(("seq", "exp"), None),
        P("exp", None, "seq"),
        P("exp", "seq", None),
    )
    return jax.shard_map(shards, mesh=mesh, in_specs=in_specs, out_specs=out_specs, check_vma=False)
```

```python
import math

import jax
import jax.numpy as jnp
from jax import lax
from jax.experimental import pallas as pl
from jax.experimental.pallas import tpu as pltpu
from jax.sharding import PartitionSpec as P

F32 = jnp.float32
BF16 = jnp.bfloat16
MESH = pl.DeviceIdType.MESH
SEQ = 8
YS = 4
XS = 4
ZS = 8
DIRECT = (0, 1, 2)
NEAR = (1, 2, ZS - 2, ZS - 1)
D = 1280
H = 640
T = 512
S = 64
VMEM = 52 * 1024 * 1024


def nn(a, b):
    return lax.dot_general(a, b, (((1,), (0,)), ((), ())), preferred_element_type=F32)


def nt(a, b):
    return lax.dot_general(a, b, (((1,), (1,)), ((), ())), preferred_element_type=F32)


def split(a):
    high = a.astype(BF16)
    return high, (a - high.astype(F32)).astype(BF16)


def thirds(column):
    value = jnp.broadcast_to(column, (8, 128))
    high, rest = split(value)
    middle, low = split(value - high.astype(F32))
    lane = lax.broadcasted_iota(jnp.int32, (8, 128), 1)
    value = jnp.where(lane == 2, low.astype(F32), 0.0)
    value = jnp.where(lane == 1, middle.astype(F32), value)
    return jnp.where(lane == 0, high.astype(F32), value)


def block(a, g):
    rows = a[8 * g : 8 * g + 8]
    return jnp.concatenate([rows[:, :H], rows[:, H:]], axis=0)


def store_blocks(ref, a):
    for g in range(SEQ):
        ref[g % 2, g // 2] = block(a, g).astype(ref.dtype)


def load_blocks(ref):
    parts = [ref[4 * (g % 2) + g // 2].astype(F32) for g in range(SEQ)]
    lo = jnp.concatenate([p[:8, :H] for p in parts], axis=0)
    hi = jnp.concatenate([p[8:, :H] for p in parts], axis=0)
    return jnp.concatenate([lo, hi], axis=1).astype(BF16)


def pair_rows(top, low):
    square = jnp.concatenate(
        [jnp.broadcast_to(top, (S, 128)), jnp.broadcast_to(low, (S, 128))], axis=0
    )
    return square.T[:8]


def columns(rows):
    return jnp.concatenate([rows] * 16, axis=0).T


def left(a, b):
    lane = lax.broadcasted_iota(jnp.int32, a.shape, 1)
    return jnp.where(lane < S, a, pltpu.roll(b, S, 1))


def merge(stats):
    lane = lax.broadcasted_iota(jnp.int32, (8, 128), 1)
    top = stats[0]
    for s in stats[1:]:
        top = jnp.maximum(top, s)
    total = jnp.zeros((8, 128), F32)
    weights = []
    for s in stats:
        w = jnp.exp(jnp.where(lane < S, s - top, 0.0))
        weights.append(w)
        total = total + pltpu.roll(s, S, 1) * w
    return jnp.where(lane < S, top, 0.0), total, weights


def kernel(
    tokens_hbm, router_hbm, w_in_hbm, w_out_hbm, grad_hbm,
    mixed_v, d_tok_v, d_rout_v, d_w_in_v, d_w_out_v,
    tok, rout, w_in, w_out, grad,
    rc0, rc1, rc2, rc3, rc4, rm0, rm1, rm2, rm3, rm4, ry0, ry1, ry2, ry3, ry4, rr0, rr1, rr2, rr3, rr4,
    es0, es1, es2, es3, es4, er0, er1, er2, er3, er4, ag0, ag1, ag2, ag3,
    st_send, st_mid, st_core, st_recv, weight,
    tc_send, tc_mid, tc_sum, ty_send, ty_recv, tz_send, tz_recv,
    in_sem, send_sem, recv_sem, hello,
):
    rc, rm = (rc0, rc1, rc2, rc3, rc4), (rm0, rm1, rm2, rm3, rm4)
    ry, rr = (ry0, ry1, ry2, ry3, ry4), (rr0, rr1, rr2, rr3, rr4)
    es, er, ag = (es0, es1, es2, es3, es4), (er0, er1, er2, er3, er4), (ag0, ag1, ag2, ag3)
    me_s = lax.axis_index("seq")
    me_n = lax.axis_index("exp")
    y = me_s // 2
    core = lax.rem(me_s, 2)
    z = me_n // XS
    x = lax.rem(me_n, XS)
    twin = me_s + 1 - 2 * core
    partner = lax.rem(me_s - z + SEQ, SEQ)
    own = lax.rem(core + z, 2)
    away = 1 - own
    mine = partner // 2

    loads = [
        pltpu.make_async_copy(src, dst, in_sem.at[i])
        for i, (src, dst) in enumerate(
            ((router_hbm, rout), (grad_hbm, grad), (w_in_hbm, w_in), (w_out_hbm, w_out))
        )
    ]
    pieces = [
        pltpu.make_async_copy(
            tokens_hbm.at[pl.ds(128 * k, 128)], tok.at[pl.ds(128 * k, 128)], in_sem.at[4 + k]
        )
        for k in range(4)
    ]
    loads[0].start()
    for piece in pieces:
        piece.start()

    barrier = pltpu.get_barrier_semaphore()

    def greet(s, n):
        pl.semaphore_signal(barrier, inc=1, device_id=(s, n), device_id_type=MESH)

    def ex_peer(k):
        return XS * partner + k

    def yx_peer(k):
        return 2 * lax.rem(y + k // XS, YS) + core, XS * z + lax.rem(x + lax.rem(k, XS), XS)

    along_x = [XS * z + lax.rem(x + k, XS) for k in range(1, XS)]
    along_z = [XS * lax.rem(z + k, ZS) + x for k in NEAR]
    for k in range(1, YS):
        greet(2 * lax.rem(y + k, YS) + core, me_n)
    for n in along_x + along_z:
        greet(me_s, n)
    greet(twin, me_n)

    def pass_on(sem, devices):
        for n in devices:
            pl.semaphore_signal(
                hello.at[sem], inc=1, device_id=(me_s, n), device_id_type=MESH
            )

    def send(src, dst, sem, s, n):
        pltpu.make_async_remote_copy(
            src_ref=src, dst_ref=dst, send_sem=send_sem.at[sem], recv_sem=recv_sem.at[sem],
            device_id=(s, n), device_id_type=MESH,
        ).start()

    def all_of(ref, sem):
        pltpu.make_async_copy(ref, ref, sem).wait()

    def arrived(ref, sem):
        all_of(ref, recv_sem.at[sem])

    def over_y(make):
        for k in (2, 1, 3):
            make(2 * lax.rem(y + k, YS) + core)

    def rs_core(i):
        send(rc[i].at[away], rm[i], 5 * i, twin, me_n)

    def rs_y_send(i):
        rr[i][y] = ry[i][mine]
        over_y(
            lambda s: send(
                ry[i].at[lax.rem(s - z + SEQ, SEQ) // 2], rr[i].at[y], 5 * i + 1, s, me_n
            )
        )

    def rs_y(i):
        arrived(rm[i], 5 * i)
        for k in range(YS):
            ry[i][k] = (rc[i][own, k].astype(F32) + rm[i][k].astype(F32)).astype(ry[i].dtype)
        rs_y_send(i)

    def rs_total(i):
        arrived(rr[i].at[pl.ds(0, YS - 1)], 5 * i + 1)
        total = rr[i][0].astype(F32)
        for k in range(1, YS):
            total = total + rr[i][k].astype(F32)
        return total

    def ex_start(i, total, extra=None):
        rows = [total[:8], total[8:]]
        if extra is not None:
            rows.append(extra)
        rows = jnp.concatenate(rows, axis=1)
        for k in range(XS):
            es[i][k] = rows[2 * k : 2 * k + 2].astype(es[i].dtype)
        for k in (2, 1, 3):
            to = lax.rem(x + k, XS)
            send(es[i].at[to], er[i].at[x], 5 * i + 2, me_s, ex_peer(to))

        @pl.when(partner != z)
        def _():
            send(es[i].at[x], er[i].at[x], 5 * i + 2, me_s, ex_peer(x))

        @pl.when(partner == z)
        def _():
            er[i][x] = es[i][x]

    def ex_rows(i):
        @pl.when(partner != z)
        def _():
            arrived(er[i], 5 * i + 2)

        @pl.when(partner == z)
        def _():
            arrived(er[i].at[pl.ds(0, XS - 1)], 5 * i + 2)

        return jnp.concatenate([er[i][k].astype(F32) for k in range(XS)], axis=0)

    def ag_start(i, rows):
        piece = jnp.concatenate([rows[:, :H], rows[:, H:D]], axis=0)
        if rows.shape[1] > D:
            extra = jnp.concatenate([rows[:, D:], jnp.zeros((8, 128), F32)], axis=0)
            piece = jnp.concatenate([piece, extra], axis=1)
        ag[i][4 * own + mine] = piece.astype(BF16)
        if i in DIRECT:
            for k in (4, 5, 3, 2, 6, 7, 1):
                send(
                    ag[i].at[4 * own + mine], ag[i].at[4 * own + mine], 5 * i + 3, lax.rem(me_s + k, SEQ), me_n
                )
        else:
            over_y(lambda s: send(ag[i].at[4 * own + mine], ag[i].at[4 * own + mine], 5 * i + 3, s, me_n))

    def ag_core(i):
        if i in DIRECT:
            return
        arrived(ag[i].at[pl.ds(0, YS - 1)], 5 * i + 3)
        half = ag[i].at[pl.ds(pl.multiple_of(4 * own, 4), 4)]
        send(half, half, 5 * i + 4, twin, me_n)

    def ag_finish(i):
        if i in DIRECT:
            arrived(ag[i].at[pl.ds(0, SEQ - 1)], 5 * i + 3)
        else:
            arrived(ag[i].at[pl.ds(0, YS)], 5 * i + 4)
        return load_blocks(ag[i])

    loads[0].wait()
    for piece in pieces:
        piece.wait()
    for load in loads[1:]:
        load.start()
    router_t = rout[...]
    logits = nt(router_t, tok[...])
    own_top = jnp.max(logits, axis=1, keepdims=True)
    own_exp = jnp.exp(logits - own_top)
    st_send[...] = pair_rows(own_top, jnp.sum(own_exp, axis=1, keepdims=True))
    exp_high, exp_low = split(own_exp)
    in_part = nn(exp_high, tok[...]) + nn(exp_low, tok[...])
    store_blocks(rc[1], in_part)

    pl.semaphore_wait(barrier, 1 + YS - 1 + XS - 1 + len(NEAR))
    rs_core(1)
    send(st_send, st_mid, 25, twin, me_n)
    pass_on(0, along_x + along_z)
    row_exp = jnp.exp(logits - jnp.max(logits, axis=0, keepdims=True))
    combine = row_exp / jnp.sum(row_exp, axis=0, keepdims=True)
    loads[1].wait()
    store_blocks(rc[0], nn(combine.astype(BF16), grad[...]))
    rs_core(0)

    arrived(st_mid, 25)
    top, total, (w_own, w_mid) = merge([st_send[...], st_mid[...]])
    st_core[...] = left(top, total)
    weight[...] = columns(left(w_own, w_mid))

    def spread(w):
        return jnp.concatenate([jnp.concatenate([w] * 5, axis=1)] * 2, axis=0)

    def weighted(i, k):
        g = pl.multiple_of(8 * (own + 2 * k), 8)
        a, b = spread(weight[pl.ds(g, 8)]), spread(weight[pl.ds(S + g, 8)])
        return rc[i][own, k].astype(F32) * a + rm[i][k].astype(F32) * b

    arrived(rm[1], 5)
    for k in range(YS):
        ry[1][k] = weighted(1, k).astype(BF16)
    st_recv[y] = st_core[...]
    over_y(lambda s: send(st_core, st_recv.at[y], 26, s, me_n))
    rs_y_send(1)
    rs_y(0)
    store_blocks(rc[4], split(in_part)[1])
    rs_core(4)
    pl.semaphore_wait(hello.at[0], XS - 1 + len(NEAR))
    pass_on(1, along_z)
    arrived(rm[4], 20)
    for k in range(YS):
        ry[4][k] = (split(weighted(1, k))[1].astype(F32) + weighted(4, k)).astype(BF16)
    rs_y_send(4)

    arrived(st_recv.at[pl.ds(0, YS - 1)], 26)
    stats = [st_recv[k] for k in range(YS)]
    top, total, ws = merge(stats)
    w = [v / total for v in ws]
    weight[...] = columns(left(w[0], w[1]))
    g = pl.multiple_of(8 * partner, 8)
    w0, w1 = weight[pl.ds(g, 8)], weight[pl.ds(S + g, 8)]
    weight[...] = columns(left(w[2], w[3]))
    w2, w3 = weight[pl.ds(g, 8)], weight[pl.ds(S + g, 8)]
    arrived(rr[1].at[pl.ds(0, YS - 1)], 6)
    total_in = jnp.zeros((16, H), F32)
    for k, v in enumerate((w0, w1, w2, w3)):
        total_in = total_in + rr[1][k].astype(F32) * spread(v)
    pl.semaphore_wait(hello.at[1], len(NEAR))
    ex_start(1, total_in)
    ex_start(0, rs_total(0))
    scale = columns(left(jnp.exp(st_send[...] - top) / total, total))[:S, :1]
    dispatch = own_exp * scale
    arrived(rr[4].at[pl.ds(0, YS - 1)], 21)
    total_low = split(total_in)[1].astype(F32)
    for k, v in enumerate((w0, w1, w2, w3)):
        total_low = total_low + rr[4][k].astype(F32) * spread(v)
    ex_start(4, total_low)

    rows_1 = ex_rows(1)
    ag_start(1, rows_1)
    ag_start(0, ex_rows(0))
    ag_core(1)
    ag_core(0)

    loads[2].wait()
    rows = ag_finish(1)
    hidden = nn(rows, w_in[...])
    cdf = 0.5 * (1.0 + lax.erf(hidden * (1.0 / math.sqrt(2.0))))
    act = hidden * cdf
    loads[3].wait()
    store_blocks(rc[3], nn(act.astype(BF16), w_out[...]))
    rs_core(3)
    pdf = jnp.exp(-0.5 * hidden * hidden) * (1.0 / math.sqrt(2.0 * math.pi))
    slope = cdf + hidden * pdf
    d_rows = ag_finish(0)
    d_hidden_b = (nt(d_rows, w_out[...]) * slope).astype(BF16)
    store_blocks(rc[2], nt(d_hidden_b, w_in[...]))
    rs_core(2)

    rs_y(3)
    rs_y(2)
    act_t = act.T.astype(BF16)
    for k in range(5):
        part = slice(128 * k, 128 * k + 128)
        d_w_out_v[part] = nn(act_t[part], d_rows).astype(BF16)
    ex_start(3, rs_total(3))
    total = rs_total(2).astype(BF16).astype(F32)
    rows_1 = rows_1 + ex_rows(4)
    column = jnp.sum(total[:8] * rows_1[:, :H] + total[8:] * rows_1[:, H:], axis=1, keepdims=True)
    ex_start(2, total, thirds(column))
    rows_t = rows.astype(F32).T.astype(BF16)
    for k in range(10):
        part = slice(128 * k, 128 * k + 128)
        d_w_in_v[part] = nn(rows_t[part], d_hidden_b).astype(BF16)
    ag_start(3, ex_rows(3))
    ag_start(2, ex_rows(2))
    ag_core(3)
    ag_core(2)

    slots_out = ag_finish(3)
    d_combine = nt(slots_out, grad[...])
    d_logit_c = combine * (d_combine - jnp.sum(combine * d_combine, axis=0, keepdims=True))
    d_slots = ag_finish(2)
    column = jnp.concatenate(
        [ag[2][4 * (g % 2) + g // 2, :8, H:].astype(F32) for g in range(SEQ)], axis=0
    )
    column = jnp.sum(column, axis=1, keepdims=True)
    d_dispatch = nt(d_slots, tok[...])
    d_logit = d_logit_c + dispatch * (d_dispatch - column)

    d_router_t = nn(d_logit.astype(BF16), tok[...])
    pair = jnp.concatenate([d_router_t, pltpu.roll(d_router_t, D - 80, 1)], axis=0).T
    for k in range(SEQ):
        tc_send[k % 2, k // 2] = pair[160 * k : 160 * k + 80]
    send(tc_send.at[1 - core], tc_mid, 27, twin, me_n)
    combine_t = combine.T.astype(BF16)
    for k in range(4):
        part = slice(128 * k, 128 * k + 128)
        mixed_v[part] = nn(combine_t[part], slots_out).astype(BF16)
    arrived(tc_mid, 27)
    for k in range(YS):
        tc_sum[k] = tc_send[core, k] + tc_mid[k]
    for k in range(YS):
        for j in range(XS):
            for i in range(5):
                ty_send[k, j, i] = tc_sum[k, pl.ds(5 * j + i, 4, stride=20), :]
    ty_recv[XS * y + x] = ty_send[y, x]

    for k in (10, 9, 11, 6, 14, 8, 2, 5, 7, 13, 15, 4, 12, 1, 3):
        s, n = yx_peer(k)
        send(ty_send.at[s // 2, lax.rem(n, XS)], ty_recv.at[XS * y + x], 28, s, n)
    weights = jnp.concatenate([dispatch, d_logit], axis=0).T.astype(BF16)
    values = jnp.concatenate([d_slots, router_t], axis=0)
    for k in range(4):
        part = slice(128 * k, 128 * k + 128)
        d_tok_v[part] = nn(weights[part], values).astype(BF16)
    arrived(ty_recv.at[pl.ds(0, YS * XS - 1)], 28)
    total = ty_recv[0]
    for k in range(1, YS * XS):
        total = total + ty_recv[k]
    tz_send[...] = jnp.zeros((ZS, 4, 128), F32)
    for k in range(3):
        first = total[2 * k]
        second = total[2 * k + 1] if k < 2 else jnp.zeros((4, 128), F32)
        for half, packed in enumerate((left(first, second), left(pltpu.roll(first, S, 1), pltpu.roll(second, S, 1)))):
            for i in range(4):
                tz_send[4 * half + i, k : k + 1] = packed[i : i + 1]
    tz_recv[z] = tz_send[z]

    for k in (4, 3, 5, 2, 6, 1, 7):
        to = lax.rem(z + k, ZS)
        send(tz_send.at[to], tz_recv.at[z], 29, me_s, XS * to + x)

    arrived(tz_recv.at[pl.ds(0, ZS - 1)], 29)
    total = tz_recv[0]
    for k in range(1, ZS):
        total = total + tz_recv[k]
    other = pltpu.roll(total, S, 1)
    for k in range(5):
        d_rout_v[k : k + 1] = (other if k % 2 else total)[k // 2 : k // 2 + 1, :S]

    for i in range(5):
        all_of(rm[i], send_sem.at[5 * i])
        all_of(rr[i].at[pl.ds(0, YS - 1)], send_sem.at[5 * i + 1])

        @pl.when(partner != z)
        def _():
            all_of(er[i], send_sem.at[5 * i + 2])

        @pl.when(partner == z)
        def _():
            all_of(er[i].at[pl.ds(0, XS - 1)], send_sem.at[5 * i + 2])

        if i == 4:
            continue
        if i in DIRECT:
            all_of(ag[i].at[pl.ds(0, SEQ - 1)], send_sem.at[5 * i + 3])
        else:
            all_of(ag[i].at[pl.ds(0, YS - 1)], send_sem.at[5 * i + 3])
            all_of(ag[i].at[pl.ds(0, YS)], send_sem.at[5 * i + 4])
    all_of(st_mid, send_sem.at[25])
    all_of(st_recv.at[pl.ds(0, YS - 1)], send_sem.at[26])
    all_of(tc_mid, send_sem.at[27])
    all_of(ty_recv.at[pl.ds(0, YS * XS - 1)], send_sem.at[28])
    all_of(tz_recv.at[pl.ds(0, ZS - 1)], send_sem.at[29])


def store(a0, a1, a2, a3, a4, b0, b1, b2, b3, b4, sem):
    copies = [
        pltpu.make_async_copy(a, b, sem.at[i])
        for i, (a, b) in enumerate(((a0, b0), (a1, b1), (a2, b2), (a3, b3), (a4, b4)))
    ]
    for copy in copies:
        copy.start()
    for copy in copies:
        copy.wait()


def shards(tokens, router, w_in, w_out, grad_out):
    any_space = pl.BlockSpec(memory_space=pl.ANY)
    dma = pltpu.SemaphoreType.DMA
    vmem = pltpu.VMEM
    wide = (0, 0, 128, 0)
    rest = (0,)
    results = pl.pallas_call(
        kernel,
        out_shape=(
            vmem((T, D), BF16),
            vmem((T, D), BF16),
            vmem((5, S), F32),
            vmem((D, H), BF16),
            vmem((H, D), BF16),
        ),
        in_specs=[any_space] * 5,
        out_specs=[pl.BlockSpec(memory_space=vmem)] * 5,
        scratch_shapes=[
            vmem((T, D), BF16),
            vmem((S, D), BF16),
            vmem((D, H), BF16),
            vmem((H, D), BF16),
            vmem((T, D), BF16),
            *[vmem((2, 4, 16, H), BF16) for _ in wide + rest],
            *[vmem((4, 16, H), BF16) for _ in wide + rest],
            *[vmem((4, 16, H), BF16) for _ in wide + rest],
            *[vmem((4, 16, H), BF16) for _ in wide + rest],
            *[vmem((XS, 2, D + w), BF16) for w in wide + rest],
            *[vmem((XS, 2, D + w), BF16) for w in wide + rest],
            *[vmem((SEQ, 16, H + w), BF16) for w in wide],
            vmem((8, 128), F32),
            vmem((8, 128), F32),
            vmem((8, 128), F32),
            vmem((YS, 8, 128), F32),
            vmem((128, 128), F32),
            vmem((2, YS, 80, 128), F32),
            vmem((YS, 80, 128), F32),
            vmem((YS, 80, 128), F32),
            vmem((YS, XS, 5, 4, 128), F32),
            vmem((YS * XS, 5, 4, 128), F32),
            vmem((ZS, 4, 128), F32),
            vmem((ZS, 4, 128), F32),
            dma((8,)), dma((30,)), dma((30,)), pltpu.SemaphoreType.REGULAR((2,)),
        ],
        compiler_params=pltpu.CompilerParams(
            collective_id=0, has_side_effects=True, vmem_limit_bytes=VMEM
        ),
    )(tokens[0], router.T, w_in[0], w_out[0], grad_out[0])
    mixed, d_tokens, d_router, d_w_in, d_w_out = pl.pallas_call(
        store,
        out_shape=tuple(jax.ShapeDtypeStruct(r.shape, r.dtype) for r in results),
        in_specs=[pl.BlockSpec(memory_space=vmem)] * 5,
        out_specs=[any_space] * 5,
        scratch_shapes=[dma((5,))],
        compiler_params=pltpu.CompilerParams(vmem_limit_bytes=4 * 1024 * 1024),
    )(*results)
    return mixed[None], d_tokens[None], d_router, d_w_in[None], d_w_out[None]


def solution(mesh):
    in_specs = (
        P("exp", "seq", None),
        P(),
        P("exp", None, "seq"),
        P("exp", "seq", None),
        P("exp", "seq", None),
    )
    out_specs = (
        P("exp", "seq", None),
        P("exp", "seq", None),
        P(("seq", "exp"), None),
        P("exp", None, "seq"),
        P("exp", "seq", None),
    )
    return jax.shard_map(shards, mesh=mesh, in_specs=in_specs, out_specs=out_specs, check_vma=False)
```
